32 devices in a mesh: dp: 8 (over y, x, core), mp: 4 (over z).
Axes of the slice: x: 2, y: 2, z: 4, core: 2. Of those that a mesh axis runs over, the one named last changes fastest.
Arguments:
- tokens: bfloat16 [16384, 8192], P('dp', 'mp'), may hold values from -24 to 24
- grid_codes: int32 [8192, 28672], P('mp', 'dp'), may hold values from 0 to 255, as said below
- residue: bfloat16 [8192, 28672], P('mp', 'dp'), may hold values from 0 to 1
- tile_spans: int32 [64, 224], P('mp', 'dp'), may hold values from 16 to 256, as said below
- tile_scales: float32 [64, 224], P('mp', 'dp'), may hold values from 0.25 to 4
- other_bits: int32 [8], replicated, may hold values from 47308 to 53043
Outputs:
- served: bfloat16 [8192, 28672], P(None, ('dp', 'mp'))
- tile_bits: float32 [64, 224], P('mp', 'dp')
The draws below stay inside these ranges and needn't reach their ends.
Inputs may be any that keep to these rules, and one draw needn't show every extreme that they name: `grid_codes`: every code lies in its tile's span around 128: 128 - tile_spans / 2 <= code < 128 + tile_spans / 2. `tile_spans`: spans are powers of two, 16 to 256, each of the five values on a fifth of the tiles.
All inputs are finite; a program needn't handle non-finite values.
Results may differ from the reference program's by a relative error of at most 0.0006.
Values may be sent and summed in bfloat16 or wider, within the bound.
No kernel may reach another device: no remote copies, remote signals or barrier semaphores. Data moves between devices by JAX's collectives and lax.ppermute only.
A program may use at most 448 MiB of HBM per device.

```python
import jax
import jax.numpy as jnp
from jax import lax

D = 8192
FF = 28672
GROUP = 128
TRIALS = 24
OTHER = 8
TOKENS = 16384
TILES = 14336


def shared_spans(key):
    order = jax.random.permutation(key, D // GROUP * (FF // GROUP))
    powers = (4 + order % 5).astype(jnp.int32)
    return jnp.left_shift(jnp.int32(1), powers).reshape(D // GROUP, FF // GROUP)


def draw_tile_spans(key, part):
    return shared_spans(key)


def draw_grid_codes(key, part):
    spans_now = shared_spans(key)
    key = jax.random.fold_in(key, 11)
    widths = jnp.broadcast_to(spans_now[:, None, :, None], (D // GROUP, GROUP, FF // GROUP, GROUP)).reshape(D, FF)
    low_edge = 128 - widths // 2
    return jax.random.randint(key, (D, FF), low_edge, low_edge + widths, dtype=jnp.int32)


def rising(count, first, last):
    ramp = jnp.arange(count, dtype=jnp.float32) / float(max(count - 1, 1))
    return jnp.exp(jnp.log(first) + ramp * (jnp.log(last) - jnp.log(first)))


def draw_tile_scales(key, part):
    key = jax.random.fold_in(key, 17)
    base = jnp.exp(jax.random.uniform(key, (D // GROUP, FF // GROUP), minval=jnp.log(0.5), maxval=jnp.log(2.0)))
    column_rise = rising(FF // GROUP, 0.6, 1.8)
    return (base * column_rise[None, :]).astype(jnp.float32)


def draw_tokens(key, part):
    key = jax.random.fold_in(key, 5)
    first, second, third = jax.random.split(key, 3)
    group_log = jax.random.uniform(first, (D // GROUP,), minval=-1.4, maxval=1.4)
    feature_log = jax.random.uniform(second, (D // GROUP, GROUP), minval=-0.35, maxval=0.35)
    feature_scale = jnp.exp(group_log[:, None] + feature_log).reshape(D)

    def one_group(group):
        group_key = jax.random.fold_in(third, group)
        key_base, key_factor, key_load, key_weight, key_sign, key_offset = jax.random.split(group_key, 6)
        base = jnp.clip(jax.random.normal(key_base, (TOKENS, GROUP)), -4.0, 4.0)
        factors = jnp.clip(jax.random.normal(key_factor, (TOKENS, 4)), -4.0, 4.0)
        factor_loadings = jax.random.uniform(key_load, (4, GROUP), minval=-1.5, maxval=1.5)
        signs = 2.0 * jax.random.randint(key_sign, (4,), 0, 2).astype(jnp.float32) - 1.0
        weights = jax.random.uniform(key_weight, (4,), minval=0.6, maxval=1.0) * signs
        offsets = 1 + jax.random.randint(key_offset, (4,), 0, GROUP - 1)
        positions = jnp.arange(GROUP, dtype=jnp.int32)
        mixed = base
        for shift_index in range(4):
            source = (positions + offsets[shift_index]) % GROUP
            mixed = mixed + weights[shift_index] * jnp.take(base, source, axis=1)
        for index_of_factor in range(4):
            mixed = mixed + factors[:, index_of_factor:index_of_factor + 1] * factor_loadings[index_of_factor][None, :]
        return mixed / 2.4
    stacked = lax.map(one_group, jnp.arange(D // GROUP, dtype=jnp.int32))
    row_rise = rising(TOKENS, 0.6, 1.8)
    values = jnp.transpose(stacked, (1, 0, 2)).reshape(TOKENS, D) * feature_scale[None, :] * row_rise[:, None]
    return jnp.clip(values, -24.0, 24.0).astype(jnp.bfloat16)


def place_ends(result, stream_key, least, largest):
    index_at = [jax.random.randint(jax.random.fold_in(stream_key, axis), (), 0, length) for axis, length in enumerate(result.shape)]
    longest = result.shape.index(max(result.shape))
    beside = index_at[:longest] + [(index_at[longest] + 1) % result.shape[longest]] + index_at[longest + 1:]
    return result.at[tuple(index_at)].set(least).at[tuple(beside)].set(largest)


def shard_levels(key, shape, pieces, smallest, top_value):
    def one(dim, shards_of):
        heights = jax.random.uniform(jax.random.fold_in(jax.random.fold_in(key, 6), dim), (shards_of,), jnp.float32, smallest / len(pieces), top_value / len(pieces))
        return jnp.repeat(jnp.exp(heights), shape[dim] // shards_of).reshape((-1,) + (1,) * (len(shape) - dim - 1))

    gain = one(*pieces[0])
    for cut in pieces[1:]:
        gain = gain * one(*cut)
    return gain


def setup_inputs(seed: int = 0) -> dict:
    keys = jax.random.split(jax.random.key(seed), 7)
    return {
        "tokens": draw_tokens(jax.random.fold_in(keys[6], 71), 0),
        "grid_codes": draw_grid_codes(jax.random.fold_in(keys[6], 71), 0),
        "residue": jnp.clip(1.0 * jax.random.uniform(keys[2], (D, FF), jnp.float32) ** shard_levels(keys[2], (D, FF), ((0, 4), (1, 8)), -0.2, 0.2), 0.0, 1.0).astype(jnp.bfloat16),
        "tile_spans": draw_tile_spans(jax.random.fold_in(keys[6], 71), 0),
        "tile_scales": draw_tile_scales(jax.random.fold_in(keys[6], 71), 0),
        "other_bits": place_ends(jax.random.randint(keys[5], (OTHER,), 33 * TILES // 10, 37 * TILES // 10 + 1), jax.random.fold_in(keys[5], 1), 33 * TILES // 10, (37 * TILES // 10 + 1) - 1).astype(jnp.int32),
    }


BIT_WIDTHS = (2, 3, 4, 8)
ERR_WEIGHT = 16.0
SOFTMAX_WARMTH = 0.03
SLOPE_LIMIT = 16.0
TARGET_BITS = 3.5


def candidates(grid_codes, residue, tile_spans, tile_scales):
    group_count, tile_count = tile_spans.shape
    shape = (group_count, GROUP, tile_count, GROUP)
    code_grid = grid_codes.reshape(shape)
    span_grid = tile_spans.reshape(group_count, 1, tile_count, 1)
    scale_grid = tile_scales.reshape(group_count, 1, tile_count, 1)
    low_edge = 128 - span_grid // 2
    values_f = code_grid.astype(jnp.float32) + residue.reshape(shape).astype(jnp.float32)
    errors_list = []
    levels_list = []
    for bit_width in BIT_WIDTHS:
        step_size = jnp.maximum(jnp.right_shift(span_grid, bit_width), 1)
        level_index = (code_grid - low_edge) // step_size
        centers = low_edge.astype(jnp.float32) + (level_index.astype(jnp.float32) + 0.5) * step_size.astype(jnp.float32)
        errors_list.append(scale_grid * (values_f - centers) / 128.0)
        levels_list.append(scale_grid * (centers / 128.0 - 1.0))
    return jnp.stack(errors_list), jnp.stack(levels_list)


def error_table(hessian, error_values):
    weighted = jnp.einsum("gij,bgjtc->bgitc", hessian, error_values, precision=lax.Precision.HIGHEST)
    return jnp.sum(error_values * weighted, axis=(2, 4)) / float(GROUP * GROUP)


def tile_probs(table, slope_now):
    column_of_bits = jnp.array(BIT_WIDTHS, dtype=jnp.float32).reshape((len(BIT_WIDTHS),) + (1,) * (table.ndim - 1))
    tile_score = ERR_WEIGHT * table + slope_now * column_of_bits
    return jax.nn.softmax(-tile_score / SOFTMAX_WARMTH, axis=0), column_of_bits


def total_rate(table, slope_now):
    probs, column_of_bits = tile_probs(table, slope_now)
    return jnp.sum(probs * column_of_bits)


def search_slope(table, goal):
    def trial(index, bounds):
        lower, upper = bounds
        middle = 0.5 * (lower + upper)
        above = total_rate(table, middle) > goal
        return (jnp.where(above, middle, lower), jnp.where(above, upper, middle))

    lower, upper = lax.fori_loop(0, TRIALS, trial, (jnp.float32(0.0), jnp.float32(SLOPE_LIMIT)))
    return 0.5 * (lower + upper)


def reference(tokens, grid_codes, residue, tile_spans, tile_scales, other_bits):
    group_total = D // GROUP

    def group_table(group):
        start = (group * GROUP).astype(jnp.int32)
        feats = lax.dynamic_slice_in_dim(tokens, start, GROUP, 1)
        hessian = jnp.dot(feats.T, feats, preferred_element_type=jnp.float32) / float(TOKENS)
        codes_rows = lax.dynamic_slice_in_dim(grid_codes, start, GROUP, 0)
        residual_rows = lax.dynamic_slice_in_dim(residue, start, GROUP, 0)
        row_of_spans = lax.dynamic_slice_in_dim(tile_spans, group.astype(jnp.int32), 1, 0)
        scales_row = lax.dynamic_slice_in_dim(tile_scales, group.astype(jnp.int32), 1, 0)
        error_values, levels = candidates(codes_rows, residual_rows, row_of_spans, scales_row)
        return error_table(hessian[None], error_values)[:, 0]

    table = jnp.transpose(lax.map(group_table, jnp.arange(group_total, dtype=jnp.int32)), (1, 0, 2))
    goal = TARGET_BITS * (OTHER + 1) * TILES - jnp.sum(other_bits).astype(jnp.float32)
    slope_final = search_slope(table, goal)
    probs, column_of_bits = tile_probs(table, slope_final)
    tile_bits = jnp.sum(probs * column_of_bits, axis=0)

    def group_mix(group):
        start = (group * GROUP).astype(jnp.int32)
        codes_rows = lax.dynamic_slice_in_dim(grid_codes, start, GROUP, 0)
        residual_rows = lax.dynamic_slice_in_dim(residue, start, GROUP, 0)
        row_of_spans = lax.dynamic_slice_in_dim(tile_spans, group.astype(jnp.int32), 1, 0)
        scales_row = lax.dynamic_slice_in_dim(tile_scales, group.astype(jnp.int32), 1, 0)
        error_values, levels = candidates(codes_rows, residual_rows, row_of_spans, scales_row)
        probs_row = lax.dynamic_slice_in_dim(probs, group.astype(jnp.int32), 1, 1)
        mixed = jnp.sum(probs_row[:, :, None, :, None] * levels, axis=0)
        return mixed.reshape(GROUP, FF).astype(jnp.bfloat16)

    served = lax.map(group_mix, jnp.arange(group_total, dtype=jnp.int32)).reshape(D, FF)
    return served, tile_bits
```

```python
import functools

import jax
import jax.numpy as jnp
from jax import lax
from jax.experimental import pallas as pl
from jax.experimental.pallas import tpu as pltpu
from jax.sharding import PartitionSpec as P

GROUP = 128
TRIALS = 24
OTHER = 8
TILES = 14336


BIT_WIDTHS = (2, 3, 4, 8)
ERR_WEIGHT = 16.0
SOFTMAX_WARMTH = 0.03
SLOPE_LIMIT = 16.0
TARGET_BITS = 3.5
MIDDLE = 128
VMEM_LIMIT = 48 * 1024 * 1024
LAST_PARTS = 2

SMALL = pl.CostEstimate(flops=1000, bytes_accessed=1000, transcendentals=0)
ANY = pl.BlockSpec(memory_space=pl.ANY)
SCALARS = pl.BlockSpec(memory_space=pltpu.SMEM)


def params_of():
    return pltpu.CompilerParams(vmem_limit_bytes=VMEM_LIMIT)


def largest_divisor(total, limit, unit):
    best = unit
    for size in range(unit, limit + 1, unit):
        if total % size == 0:
            best = size
    return best


def cast_kernel(where_ref, codes_ref, *rest):
    out_ref = rest[-1]
    out_ref[...] = (codes_ref[...] - MIDDLE).astype(jnp.float32).astype(jnp.bfloat16)


def codes_for(grid_codes, dest, width, first_row, row_count, after):
    if width % 128:
        part = lax.dynamic_slice(grid_codes, (jnp.int32(first_row), dest * width), (row_count, width))
        return (part - MIDDLE).astype(jnp.bfloat16)
    block = largest_divisor(row_count, 256, 16)
    first_block = first_row // block
    return pl.pallas_call(
        cast_kernel,
        out_shape=jax.ShapeDtypeStruct((row_count, width), jnp.bfloat16),
        grid_spec=pltpu.PrefetchScalarGridSpec(
            num_scalar_prefetch=1,
            grid=(row_count // block,),
            in_specs=[pl.BlockSpec((block, width), lambda i, where: (first_block + i, where[0]))] + [ANY] * len(after),
            out_specs=pl.BlockSpec((block, width), lambda i, where: (i, 0)),
        ),
        compiler_params=params_of(),
        cost_estimate=SMALL,
        name="cast_codes",
    )(dest.reshape(1), grid_codes, *after)


def gram_kernel(tokens_ref, *rest):
    out_ref = rest[-1]
    feats = tokens_ref[...]
    out_ref[0] = lax.dot_general(feats, feats, (((0,), (0,)), ((), ())), preferred_element_type=jnp.float32)


def gram_blocks(tokens, after):
    tok_count, width_local = tokens.shape
    group_count = width_local // GROUP
    return pl.pallas_call(
        gram_kernel,
        out_shape=jax.ShapeDtypeStruct((group_count, GROUP, GROUP), jnp.float32),
        grid=(group_count,),
        in_specs=[pl.BlockSpec((tok_count, GROUP), lambda g: (0, g))] + [ANY] * len(after),
        out_specs=pl.BlockSpec((1, GROUP, GROUP), lambda g: (g, 0, 0)),
        compiler_params=params_of(),
        cost_estimate=SMALL,
        name="gram",
    )(tokens, *after)


def table_kernel(token_total, chunk, spans_ref, hessian_ref, codes_ref, residue_ref, out_ref, sums_ref):
    group = pl.program_id(0)
    width = codes_ref.shape[1]
    tile_count = width // GROUP
    per_chunk = chunk // GROUP
    hessian = hessian_ref[0] / token_total
    high = hessian.astype(jnp.bfloat16)
    high_f = high.astype(jnp.float32)
    low = (hessian - high_f).astype(jnp.bfloat16)
    both = jnp.concatenate([high, low], axis=1)
    half_rows = 0.5 * jnp.sum(high_f + low.astype(jnp.float32), axis=1, keepdims=True)
    sums_ref[...] = jnp.zeros_like(sums_ref)

    def weigh(values):
        return jnp.dot(both, jnp.concatenate([values, values], axis=0), preferred_element_type=jnp.float32)

    def one_chunk(index, carry):
        start = pl.multiple_of(index * chunk, chunk)
        codes = codes_ref[:, pl.ds(start, chunk)]
        rest = residue_ref[:, pl.ds(start, chunk)]
        rest_weighted = weigh(rest) - half_rows
        rest_centred = rest.astype(jnp.float32) - 0.5
        spans = [spans_ref[group, index * per_chunk + t] for t in range(per_chunk)]
        for row, bit_width in enumerate(BIT_WIDTHS[:-1]):
            pieces = []
            for t in range(per_chunk):
                mask = jnp.right_shift(spans[t], bit_width) - 1
                inside = jnp.bitwise_and(codes[:, t * GROUP:(t + 1) * GROUP], mask)
                pieces.append(inside.astype(jnp.float32) - 0.5 * mask.astype(jnp.float32))
            offset = jnp.concatenate(pieces, axis=1)
            weighted = weigh(offset.astype(jnp.bfloat16)) + rest_weighted
            sums_ref[row:row + 1, pl.ds(start, chunk)] = jnp.sum((offset + rest_centred) * weighted, axis=0, keepdims=True)
        last = len(BIT_WIDTHS) - 1
        sums_ref[last:last + 1, pl.ds(start, chunk)] = jnp.sum(rest_centred * rest_weighted, axis=0, keepdims=True)
        return carry

    lax.fori_loop(0, width // chunk, one_chunk, 0)
    lanes = lax.broadcasted_iota(jnp.int32, out_ref.shape[1:], 1)
    totals = jnp.zeros(out_ref.shape[1:], jnp.float32)
    for tile in range(tile_count):
        total = jnp.sum(sums_ref[:, tile * GROUP:(tile + 1) * GROUP], axis=1, keepdims=True)
        totals = jnp.where(lanes == tile, total, totals)
    out_ref[0] = totals


def error_sums(hessian, grid_codes, residue, tile_spans, token_total):
    group_count, tile_count = tile_spans.shape
    width = grid_codes.shape[1]
    chunk = 256 if width % 256 == 0 else GROUP
    lanes = -(-tile_count // 128) * 128
    return pl.pallas_call(
        functools.partial(table_kernel, float(token_total), chunk),
        out_shape=jax.ShapeDtypeStruct((group_count, 8, lanes), jnp.float32),
        grid_spec=pltpu.PrefetchScalarGridSpec(
            num_scalar_prefetch=1,
            grid=(group_count,),
            in_specs=[
                pl.BlockSpec((1, GROUP, GROUP), lambda g, spans: (g, 0, 0)),
                pl.BlockSpec((GROUP, width), lambda g, spans: (g, 0)),
                pl.BlockSpec((GROUP, width), lambda g, spans: (g, 0)),
            ],
            out_specs=pl.BlockSpec((1, 8, lanes), lambda g, spans: (g, 0, 0)),
            scratch_shapes=[pltpu.VMEM((8, width), jnp.float32)],
        ),
        compiler_params=params_of(),
        cost_estimate=SMALL,
        name="error_table",
    )(tile_spans, hessian, grid_codes, residue)


def probs_of(tables, slope_now):
    scores = [-(ERR_WEIGHT * t + slope_now * float(b)) / SOFTMAX_WARMTH for t, b in zip(tables, BIT_WIDTHS)]
    top = functools.reduce(jnp.maximum, scores)
    raised = [jnp.exp(score - top) for score in scores]
    total = functools.reduce(jnp.add, raised)
    return raised, total


def bits_of(tables, slope_now):
    raised, total = probs_of(tables, slope_now)
    return functools.reduce(jnp.add, [r * float(b) for r, b in zip(raised, BIT_WIDTHS)]) / total


def slope_kernel(goal_ref, me_ref, all_ref, mine_ref, coef_ref, bits_ref, tables_ref):
    bit_count = len(BIT_WIDTHS)
    for row in range(bit_count):
        tables_ref[row] = all_ref[:, row, :]
    goal = goal_ref[0]

    def trial(index, bounds):
        lower, upper = bounds
        middle = 0.5 * (lower + upper)
        rate = jnp.sum(bits_of([tables_ref[row] for row in range(bit_count)], middle))
        above = rate > goal
        return (jnp.where(above, middle, lower), jnp.where(above, upper, middle))

    lower, upper = lax.fori_loop(0, TRIALS, trial, (jnp.float32(0.0), jnp.float32(SLOPE_LIMIT)))
    slope_final = 0.5 * (lower + upper)

    tables = [mine_ref[row] for row in range(bit_count)]
    spans, scales = mine_ref[bit_count], mine_ref[bit_count + 1]
    bits_ref[...] = bits_of(tables, slope_final)
    raised, total = probs_of(tables, slope_final)
    unit = scales / 128.0
    offset = jnp.zeros_like(unit)
    gains = []
    inverses = []
    for weight, bit_width in zip(raised, BIT_WIDTHS):
        prob = weight / total
        step = jnp.maximum(spans * (0.5 ** bit_width), 1.0)
        gains.append(unit * prob * step)
        inverses.append(1.0 / step)
        offset = offset + 0.5 * unit * prob * step
    rows = [gains[-1], offset] + gains[:-1] + inverses[:-1]
    stacked = jnp.concatenate(rows, axis=0)
    group_total, _, width = coef_ref.shape
    tile_count = unit.shape[1]
    tile = lax.broadcasted_iota(jnp.int32, (tile_count, width), 0)
    column = lax.broadcasted_iota(jnp.int32, (tile_count, width), 1) + me_ref[0] * width
    first = tile * GROUP
    spread = jnp.where((column >= first) & (column < first + GROUP), 1.0, 0.0)
    columns = jnp.dot(stacked, spread, precision=lax.Precision.HIGHEST, preferred_element_type=jnp.float32)
    for row in range(len(rows)):
        coef_ref[:, row, :] = columns[row * group_total:(row + 1) * group_total]


def find_slope(goal, me, gathered, mine, width):
    device_count, _, tile_local = gathered.shape
    _, group_total, tile_count = mine.shape
    whole = pl.BlockSpec(memory_space=pltpu.VMEM)
    return pl.pallas_call(
        slope_kernel,
        out_shape=(
            jax.ShapeDtypeStruct((group_total, 8, width), jnp.float32),
            jax.ShapeDtypeStruct((group_total, tile_count), jnp.float32),
        ),
        in_specs=[SCALARS, SCALARS, whole, whole],
        out_specs=(whole, whole),
        scratch_shapes=[pltpu.VMEM((len(BIT_WIDTHS), device_count, tile_local), jnp.float32)],
        compiler_params=params_of(),
        cost_estimate=SMALL,
        name="find_slope",
    )(goal.reshape(1), me.reshape(1), gathered, mine)


def serve_kernel(groups, where_ref, codes_ref, coef_ref, *rest):
    out_ref = rest[-1]
    for group in range(groups):
        rows = pl.ds(group * GROUP, GROUP)
        codes = codes_ref[rows, :]
        if codes.dtype == jnp.int32:
            codes = codes - MIDDLE
        codes = codes.astype(jnp.float32)
        mixed = coef_ref[group, 1:2, :] + coef_ref[group, 0:1, :] * codes
        for row in range(len(BIT_WIDTHS) - 1):
            gain = coef_ref[group, 2 + row:3 + row, :]
            inverse = coef_ref[group, 5 + row:6 + row, :]
            mixed = mixed + gain * jnp.floor(codes * inverse)
        out_ref[rows, :] = mixed.astype(jnp.bfloat16)


def serve(codes, column_block, coef, source, rows_each, first_row, row_count, served):
    group_total, _, width = coef.shape
    groups = largest_divisor(row_count // GROUP, 2, 1)
    block = groups * GROUP
    first_block = first_row // block
    steps = rows_each // block
    where = jnp.stack([source, column_block])
    whole_codes = codes.shape[0] != row_count or codes.shape[1] != width
    code_first = first_block if whole_codes else 0
    before = [] if served is None else [served]
    return pl.pallas_call(
        functools.partial(serve_kernel, groups),
        out_shape=jax.ShapeDtypeStruct((group_total * GROUP, width), jnp.bfloat16),
        grid_spec=pltpu.PrefetchScalarGridSpec(
            num_scalar_prefetch=1,
            grid=(row_count // block,),
            in_specs=[
                pl.BlockSpec((block, width), lambda i, where: (code_first + i, where[1])),
                pl.BlockSpec((groups, 8, width), lambda i, where: (where[0] * steps + first_block + i, 0, 0)),
            ] + [ANY] * len(before),
            out_specs=pl.BlockSpec((block, width), lambda i, where: (where[0] * steps + first_block + i, 0)),
        ),
        input_output_aliases={3: 0} if before else {},
        compiler_params=params_of(),
        cost_estimate=SMALL,
        name="serve",
    )(where, codes, coef, *before)


def local(tokens, grid_codes, residue, tile_spans, tile_scales, other_bits):
    dp_count, mp_count = lax.axis_size("dp"), lax.axis_size("mp")
    me = lax.axis_index("mp").astype(jnp.int32)
    none = jnp.int32(0)
    rows, columns = grid_codes.shape
    width = columns // mp_count
    group_count, tile_count = tile_spans.shape
    group_total = group_count * mp_count
    token_total = tokens.shape[0] * dp_count

    shifts = sorted(range(1, mp_count), key=lambda k: -min(k, mp_count - k))
    parts = []
    for place, shift in enumerate(shifts):
        pieces = LAST_PARTS if place == len(shifts) - 1 and group_count % LAST_PARTS == 0 else 1
        for piece in range(pieces):
            parts.append((shift, piece * (rows // pieces), rows // pieces))
    arrived = []
    gram = None
    for shift, first_row, row_count in parts:
        dest = lax.rem(me + shift, mp_count)
        after = [] if gram is None else [gram]
        sent = codes_for(grid_codes, dest, width, first_row, row_count, after)
        if gram is None:
            gram = gram_blocks(tokens, [sent])
        arrived.append(lax.ppermute(sent, "mp", [(z, (z + shift) % mp_count) for z in range(mp_count)]))

    hessian = lax.psum(gram, "dp")
    sums = error_sums(hessian, grid_codes, residue, tile_spans, token_total)
    unit = tile_scales / 128.0
    bit_count = len(BIT_WIDTHS)
    table = sums[:, :bit_count, :tile_count] * (unit * unit / float(GROUP * GROUP))[:, None, :]
    mine = jnp.concatenate(
        [
            jnp.transpose(table, (1, 0, 2)).reshape(bit_count, -1),
            tile_spans.astype(jnp.float32).reshape(1, -1),
            tile_scales.reshape(1, -1),
        ]
    )
    gathered = lax.all_gather(mine, ("dp", "mp"))
    goal = TARGET_BITS * (OTHER + 1) * TILES - jnp.sum(other_bits).astype(jnp.float32)
    line = lax.dynamic_slice_in_dim(gathered, lax.axis_index("dp") * mp_count, mp_count, 0)
    line = line.reshape(mp_count, bit_count + 2, group_count, tile_count)
    line = jnp.transpose(line, (1, 0, 2, 3)).reshape(bit_count + 2, group_total, tile_count)
    coef, bits = find_slope(goal, me, gathered, line, width)
    tile_bits = lax.dynamic_slice_in_dim(bits, me * group_count, group_count, 0)

    if width % 128:
        own = codes_for(grid_codes, me, width, 0, rows, [])
        served = serve(own, none, coef, me, rows, 0, rows, None)
    else:
        served = serve(grid_codes, me, coef, me, rows, 0, rows, None)
    for (shift, first_row, row_count), codes in zip(parts, arrived):
        source = lax.rem(me + mp_count - shift, mp_count)
        served = serve(codes, none, coef, source, rows, first_row, row_count, served)
    return (served, tile_bits)


def solution(mesh):
    placed = (P("dp", "mp"), P("mp", "dp"), P("mp", "dp"), P("mp", "dp"), P("mp", "dp"), P())
    return jax.shard_map(
        local,
        mesh=mesh,
        in_specs=placed,
        out_specs=(P(None, ("dp", "mp")), P("mp", "dp")),
        check_vma=False,
    )
```

```python
import functools

import jax
import jax.numpy as jnp
from jax import lax
from jax.experimental import pallas as pl
from jax.experimental.pallas import tpu as pltpu
from jax.sharding import PartitionSpec as P

GROUP = 128
TRIALS = 24
OTHER = 8
TILES = 14336


BIT_WIDTHS = (2, 3, 4, 8)
ERR_WEIGHT = 16.0
SOFTMAX_WARMTH = 0.03
SLOPE_LIMIT = 16.0
TARGET_BITS = 3.5
MIDDLE = 128
VMEM_LIMIT = 48 * 1024 * 1024

SMALL = pl.CostEstimate(flops=1000, bytes_accessed=1000, transcendentals=0)
ANY = pl.BlockSpec(memory_space=pl.ANY)
SCALARS = pl.BlockSpec(memory_space=pltpu.SMEM)


def params_of():
    return pltpu.CompilerParams(vmem_limit_bytes=VMEM_LIMIT)


def largest_divisor(total, limit, unit):
    best = unit
    for size in range(unit, limit + 1, unit):
        if total % size == 0:
            best = size
    return best


def cast_kernel(where_ref, codes_ref, *rest):
    out_ref = rest[-1]
    out_ref[...] = (codes_ref[...] - MIDDLE).astype(jnp.float32).astype(jnp.bfloat16)


def codes_for(grid_codes, dest, width, first_row, row_count, after):
    if width % 128:
        part = lax.dynamic_slice(grid_codes, (jnp.int32(first_row), dest * width), (row_count, width))
        return (part - MIDDLE).astype(jnp.bfloat16)
    block = largest_divisor(row_count, 256, 16)
    first_block = first_row // block
    return pl.pallas_call(
        cast_kernel,
        out_shape=jax.ShapeDtypeStruct((row_count, width), jnp.bfloat16),
        grid_spec=pltpu.PrefetchScalarGridSpec(
            num_scalar_prefetch=1,
            grid=(row_count // block,),
            in_specs=[pl.BlockSpec((block, width), lambda i, where: (first_block + i, where[0]))] + [ANY] * len(after),
            out_specs=pl.BlockSpec((block, width), lambda i, where: (i, 0)),
        ),
        compiler_params=params_of(),
        cost_estimate=SMALL,
        name="cast_codes",
    )(dest.reshape(1), grid_codes, *after)


def gram_kernel(tokens_ref, *rest):
    out_ref = rest[-1]
    feats = tokens_ref[...]
    out_ref[0] = lax.dot_general(feats, feats, (((0,), (0,)), ((), ())), preferred_element_type=jnp.float32)


def gram_blocks(tokens, after):
    tok_count, width_local = tokens.shape
    group_count = width_local // GROUP
    return pl.pallas_call(
        gram_kernel,
        out_shape=jax.ShapeDtypeStruct((group_count, GROUP, GROUP), jnp.float32),
        grid=(group_count,),
        in_specs=[pl.BlockSpec((tok_count, GROUP), lambda g: (0, g))] + [ANY] * len(after),
        out_specs=pl.BlockSpec((1, GROUP, GROUP), lambda g: (g, 0, 0)),
        compiler_params=params_of(),
        cost_estimate=SMALL,
        name="gram",
    )(tokens, *after)


def table_kernel(token_total, chunk, spans_ref, hessian_ref, codes_ref, residue_ref, factor_ref, added_ref, out_ref, sums_ref):
    group = pl.program_id(0)
    width = codes_ref.shape[1]
    tile_count = width // GROUP
    per_chunk = chunk // GROUP
    hessian = hessian_ref[0] / token_total
    high = hessian.astype(jnp.bfloat16)
    high_f = high.astype(jnp.float32)
    low = (hessian - high_f).astype(jnp.bfloat16)
    both = jnp.concatenate([high, low], axis=1)
    half_rows = 0.5 * jnp.sum(high_f + low.astype(jnp.float32), axis=1, keepdims=True)
    sums_ref[...] = jnp.zeros_like(sums_ref)

    def weigh(values):
        return jnp.dot(both, jnp.concatenate([values, values], axis=0), preferred_element_type=jnp.float32)

    def one_chunk(index, carry):
        start = pl.multiple_of(index * chunk, chunk)
        codes = codes_ref[:, pl.ds(start, chunk)]
        rest = residue_ref[:, pl.ds(start, chunk)]
        rest_weighted = weigh(rest) - half_rows
        rest_centred = rest.astype(jnp.float32) - 0.5
        spans = [spans_ref[group, index * per_chunk + t] for t in range(per_chunk)]
        for row, bit_width in enumerate(BIT_WIDTHS[:-1]):
            pieces = []
            for t in range(per_chunk):
                mask = jnp.right_shift(spans[t], bit_width) - 1
                inside = jnp.bitwise_and(codes[:, t * GROUP:(t + 1) * GROUP], mask)
                pieces.append(inside.astype(jnp.float32) - 0.5 * mask.astype(jnp.float32))
            offset = jnp.concatenate(pieces, axis=1)
            weighted = weigh(offset.astype(jnp.bfloat16)) + rest_weighted
            sums_ref[row:row + 1, pl.ds(start, chunk)] = jnp.sum((offset + rest_centred) * weighted, axis=0, keepdims=True)
        last = len(BIT_WIDTHS) - 1
        sums_ref[last:last + 1, pl.ds(start, chunk)] = jnp.sum(rest_centred * rest_weighted, axis=0, keepdims=True)
        return carry

    lax.fori_loop(0, width // chunk, one_chunk, 0)
    lanes = lax.broadcasted_iota(jnp.int32, out_ref.shape[1:], 1)
    totals = jnp.zeros(out_ref.shape[1:], jnp.float32)
    for tile in range(tile_count):
        total = jnp.sum(sums_ref[:, tile * GROUP:(tile + 1) * GROUP], axis=1, keepdims=True)
        totals = jnp.where(lanes == tile, total, totals)
    out_ref[0] = totals * factor_ref[0] + added_ref[0]


def error_table(hessian, grid_codes, residue, tile_spans, tile_scales, token_total):
    group_count, tile_count = tile_spans.shape
    width = grid_codes.shape[1]
    chunk = 256 if width % 256 == 0 else GROUP
    lanes = -(-tile_count // 128) * 128
    bit_count = len(BIT_WIDTHS)
    unit = tile_scales / 128.0
    factor = jnp.broadcast_to((unit * unit / float(GROUP * GROUP))[:, None, :], (group_count, bit_count, tile_count))
    factor = jnp.pad(factor, ((0, 0), (0, 8 - bit_count), (0, lanes - tile_count)))
    added = jnp.stack([tile_spans.astype(jnp.float32), tile_scales], axis=1)
    added = jnp.pad(added, ((0, 0), (bit_count, 6 - bit_count), (0, lanes - tile_count)))
    rows = pl.BlockSpec((1, 8, lanes), lambda g, spans: (g, 0, 0))
    return pl.pallas_call(
        functools.partial(table_kernel, float(token_total), chunk),
        out_shape=jax.ShapeDtypeStruct((group_count, 8, lanes), jnp.float32),
        grid_spec=pltpu.PrefetchScalarGridSpec(
            num_scalar_prefetch=1,
            grid=(group_count,),
            in_specs=[
                pl.BlockSpec((1, GROUP, GROUP), lambda g, spans: (g, 0, 0)),
                pl.BlockSpec((GROUP, width), lambda g, spans: (g, 0)),
                pl.BlockSpec((GROUP, width), lambda g, spans: (g, 0)),
                rows,
                rows,
            ],
            out_specs=rows,
            scratch_shapes=[pltpu.VMEM((8, width), jnp.float32)],
        ),
        compiler_params=params_of(),
        cost_estimate=SMALL,
        name="error_table",
    )(tile_spans, hessian, grid_codes, residue, factor, added)


def probs_of(tables, slope_now):
    scores = [-(ERR_WEIGHT * t + slope_now * float(b)) / SOFTMAX_WARMTH for t, b in zip(tables, BIT_WIDTHS)]
    top = functools.reduce(jnp.maximum, scores)
    raised = [jnp.exp(score - top) for score in scores]
    total = functools.reduce(jnp.add, raised)
    return raised, total


def bits_of(tables, slope_now):
    raised, total = probs_of(tables, slope_now)
    return functools.reduce(jnp.add, [r * float(b) for r, b in zip(raised, BIT_WIDTHS)]) / total


def slope_kernel(tile_count, pack, goal_ref, me_ref, all_ref, coef_ref, bits_ref, tables_ref):
    bit_count = len(BIT_WIDTHS)
    lanes = all_ref.shape[2]
    pitch = lanes // pack
    packed_rows = tables_ref.shape[1]
    for row in range(bit_count):
        packed = all_ref[:packed_rows, row, :]
        for place in range(1, pack):
            part = all_ref[place * packed_rows:(place + 1) * packed_rows, row, :]
            packed = packed + pltpu.roll(part, place * pitch, 1)
        tables_ref[row] = packed
    goal = goal_ref[0]
    lane = lax.broadcasted_iota(jnp.int32, (packed_rows, lanes), 1)
    held = lax.rem(lane, jnp.int32(pitch)) < tile_count

    def trial(index, bounds):
        lower, upper = bounds
        middle = 0.5 * (lower + upper)
        bits = bits_of([tables_ref[row] for row in range(bit_count)], middle)
        above = jnp.sum(jnp.where(held, bits, 0.0)) > goal
        return (jnp.where(above, middle, lower), jnp.where(above, upper, middle))

    lower, upper = lax.fori_loop(0, TRIALS, trial, (jnp.float32(0.0), jnp.float32(SLOPE_LIMIT)))
    slope_final = 0.5 * (lower + upper)

    group_total, _, width = coef_ref.shape
    mine = pl.ds(me_ref[0] * group_total, group_total)
    tables = [all_ref[mine, row, :] for row in range(bit_count)]
    spans, scales = all_ref[mine, bit_count, :], all_ref[mine, bit_count + 1, :]
    bits_ref[...] = bits_of(tables, slope_final)
    raised, total = probs_of(tables, slope_final)
    unit = scales / 128.0
    offset = jnp.zeros_like(unit)
    gains = []
    inverses = []
    for weight, bit_width in zip(raised, BIT_WIDTHS):
        prob = weight / total
        step = jnp.maximum(spans * (0.5 ** bit_width), 1.0)
        gains.append(unit * prob * step)
        inverses.append(1.0 / step)
        offset = offset + 0.5 * unit * prob * step
    rows = [gains[-1], offset] + gains[:-1] + inverses[:-1]
    stacked = jnp.concatenate(rows, axis=0)
    tile = lax.broadcasted_iota(jnp.int32, (lanes, width), 0)
    column = lax.broadcasted_iota(jnp.int32, (lanes, width), 1) + me_ref[1] * width
    first = tile * GROUP
    spread = jnp.where((column >= first) & (column < first + GROUP), 1.0, 0.0)
    columns = jnp.dot(stacked, spread, precision=lax.Precision.HIGHEST, preferred_element_type=jnp.float32)
    for row in range(len(rows)):
        coef_ref[:, row, :] = columns[row * group_total:(row + 1) * group_total]


def find_slope(goal, me, gathered, group_total, tile_count, width):
    group_all, _, lanes = gathered.shape
    pack = 4 if tile_count <= lanes // 4 and group_all % 32 == 0 else 1
    whole = pl.BlockSpec(memory_space=pltpu.VMEM)
    return pl.pallas_call(
        functools.partial(slope_kernel, tile_count, pack),
        out_shape=(
            jax.ShapeDtypeStruct((group_total, 8, width), jnp.float32),
            jax.ShapeDtypeStruct((group_total, lanes), jnp.float32),
        ),
        in_specs=[SCALARS, SCALARS, whole],
        out_specs=(whole, whole),
        scratch_shapes=[pltpu.VMEM((len(BIT_WIDTHS), group_all // pack, lanes), jnp.float32)],
        compiler_params=params_of(),
        cost_estimate=SMALL,
        name="find_slope",
    )(goal.reshape(1), me, gathered)


def serve_kernel(groups, where_ref, codes_ref, coef_ref, *rest):
    out_ref = rest[-1]
    for group in range(groups):
        rows = pl.ds(group * GROUP, GROUP)
        codes = codes_ref[rows, :]
        if codes.dtype == jnp.int32:
            codes = codes - MIDDLE
        codes = codes.astype(jnp.float32)
        mixed = coef_ref[group, 1:2, :] + coef_ref[group, 0:1, :] * codes
        for row in range(len(BIT_WIDTHS) - 1):
            gain = coef_ref[group, 2 + row:3 + row, :]
            inverse = coef_ref[group, 5 + row:6 + row, :]
            mixed = mixed + gain * jnp.floor(codes * inverse)
        out_ref[rows, :] = mixed.astype(jnp.bfloat16)


def serve(codes, column_block, coef, source, rows_each, first_row, row_count, served):
    group_total, _, width = coef.shape
    groups = largest_divisor(row_count // GROUP, 2, 1)
    block = groups * GROUP
    first_block = first_row // block
    steps = rows_each // block
    where = jnp.stack([source, column_block])
    whole_codes = codes.shape[0] != row_count or codes.shape[1] != width
    code_first = first_block if whole_codes else 0
    before = [] if served is None else [served]
    return pl.pallas_call(
        functools.partial(serve_kernel, groups),
        out_shape=jax.ShapeDtypeStruct((group_total * GROUP, width), jnp.bfloat16),
        grid_spec=pltpu.PrefetchScalarGridSpec(
            num_scalar_prefetch=1,
            grid=(row_count // block,),
            in_specs=[
                pl.BlockSpec((block, width), lambda i, where: (code_first + i, where[1])),
                pl.BlockSpec((groups, 8, width), lambda i, where: (where[0] * steps + first_block + i, 0, 0)),
            ] + [ANY] * len(before),
            out_specs=pl.BlockSpec((block, width), lambda i, where: (where[0] * steps + first_block + i, 0)),
        ),
        input_output_aliases={3: 0} if before else {},
        compiler_params=params_of(),
        cost_estimate=SMALL,
        name="serve",
    )(where, codes, coef, *before)


def local(tokens, grid_codes, residue, tile_spans, tile_scales, other_bits):
    dp_count, mp_count = lax.axis_size("dp"), lax.axis_size("mp")
    me = lax.axis_index("mp").astype(jnp.int32)
    none = jnp.int32(0)
    rows, columns = grid_codes.shape
    width = columns // mp_count
    group_count, tile_count = tile_spans.shape
    group_total = group_count * mp_count
    token_total = tokens.shape[0] * dp_count

    shifts = sorted(range(1, mp_count), key=lambda k: -min(k, mp_count - k))
    short = rows // 4 if group_count % 4 == 0 else rows
    parts = []
    for place, shift in enumerate(shifts):
        cuts = [0, rows]
        if place == len(shifts) - 1:
            cuts = sorted({0, rows - short, rows})
        parts += [(shift, first, end - first) for first, end in zip(cuts, cuts[1:]) if end > first]
    arrived = []
    gram = None
    for shift, first_row, row_count in parts:
        dest = lax.rem(me + shift, mp_count)
        after = [] if gram is None else [gram]
        sent = codes_for(grid_codes, dest, width, first_row, row_count, after)
        if gram is None:
            gram = gram_blocks(tokens, [sent])
        arrived.append(lax.ppermute(sent, "mp", [(z, (z + shift) % mp_count) for z in range(mp_count)]))

    hessian = lax.psum(gram, "dp")
    table = error_table(hessian, grid_codes, residue, tile_spans, tile_scales, token_total)
    gathered = lax.all_gather(table, ("dp", "mp"), tiled=True)
    goal = TARGET_BITS * (OTHER + 1) * TILES - jnp.sum(other_bits).astype(jnp.float32)
    places = jnp.stack([lax.axis_index("dp").astype(jnp.int32), me])
    coef, bits = find_slope(goal, places, gathered, group_total, tile_count, width)
    tile_bits = lax.dynamic_slice(bits, (me * group_count, none), (group_count, tile_count))

    if width % 128:
        own = codes_for(grid_codes, me, width, 0, rows, [])
        served = serve(own, none, coef, me, rows, 0, rows, None)
    else:
        served = serve(grid_codes, me, coef, me, rows, 0, rows, None)
    for (shift, first_row, row_count), codes in zip(parts, arrived):
        source = lax.rem(me + mp_count - shift, mp_count)
        served = serve(codes, none, coef, source, rows, first_row, row_count, served)
    return (served, tile_bits)


def solution(mesh):
    placed = (P("dp", "mp"), P("mp", "dp"), P("mp", "dp"), P("mp", "dp"), P("mp", "dp"), P())
    return jax.shard_map(
        local,
        mesh=mesh,
        in_specs=placed,
        out_specs=(P(None, ("dp", "mp")), P("mp", "dp")),
        check_vma=False,
    )
```

```python
import functools

import jax
import jax.numpy as jnp
from jax import lax
from jax.experimental import pallas as pl
from jax.experimental.pallas import tpu as pltpu
from jax.sharding import PartitionSpec as P

GROUP = 128
TRIALS = 24
OTHER = 8
TILES = 14336


BIT_WIDTHS = (2, 3, 4, 8)
ERR_WEIGHT = 16.0
SOFTMAX_WARMTH = 0.03
SLOPE_LIMIT = 16.0
TARGET_BITS = 3.5
MIDDLE = 128
VMEM_LIMIT = 48 * 1024 * 1024

SMALL = pl.CostEstimate(flops=1000, bytes_accessed=1000, transcendentals=0)
ANY = pl.BlockSpec(memory_space=pl.ANY)
SCALARS = pl.BlockSpec(memory_space=pltpu.SMEM)


def params_of():
    return pltpu.CompilerParams(vmem_limit_bytes=VMEM_LIMIT)


def largest_divisor(total, limit, unit):
    best = unit
    for size in range(unit, limit + 1, unit):
        if total % size == 0:
            best = size
    return best


def touch_kernel(*refs):
    pass


def once_there(value, after):
    return pl.pallas_call(
        touch_kernel,
        out_shape=jax.ShapeDtypeStruct(value.shape, value.dtype),
        in_specs=[ANY] * (1 + len(after)),
        out_specs=ANY,
        input_output_aliases={0: 0},
        compiler_params=params_of(),
        cost_estimate=SMALL,
        name="once_there",
    )(value, *after)


def cast_kernel(where_ref, codes_ref, *rest):
    out_ref = rest[-1]
    out_ref[...] = (codes_ref[...] - MIDDLE).astype(jnp.float32).astype(jnp.bfloat16)


def codes_for(grid_codes, dest, width, first_row, row_count, after):
    if width % 128:
        part = lax.dynamic_slice(grid_codes, (jnp.int32(first_row), dest * width), (row_count, width))
        return (part - MIDDLE).astype(jnp.bfloat16)
    block = largest_divisor(row_count, 256, 16)
    first_block = first_row // block
    return pl.pallas_call(
        cast_kernel,
        out_shape=jax.ShapeDtypeStruct((row_count, width), jnp.bfloat16),
        grid_spec=pltpu.PrefetchScalarGridSpec(
            num_scalar_prefetch=1,
            grid=(row_count // block,),
            in_specs=[pl.BlockSpec((block, width), lambda i, where: (first_block + i, where[0]))] + [ANY] * len(after),
            out_specs=pl.BlockSpec((block, width), lambda i, where: (i, 0)),
        ),
        compiler_params=params_of(),
        cost_estimate=SMALL,
        name="cast_codes",
    )(dest.reshape(1), grid_codes, *after)


def gram_kernel(tokens_ref, *rest):
    out_ref = rest[-1]
    feats = tokens_ref[...]
    out_ref[0] = lax.dot_general(feats, feats, (((0,), (0,)), ((), ())), preferred_element_type=jnp.float32)


def gram_blocks(tokens, after):
    tok_count, width_local = tokens.shape
    group_count = width_local // GROUP
    return pl.pallas_call(
        gram_kernel,
        out_shape=jax.ShapeDtypeStruct((group_count, GROUP, GROUP), jnp.float32),
        grid=(group_count,),
        in_specs=[pl.BlockSpec((tok_count, GROUP), lambda g: (0, g))] + [ANY] * len(after),
        out_specs=pl.BlockSpec((1, GROUP, GROUP), lambda g: (g, 0, 0)),
        compiler_params=params_of(),
        cost_estimate=SMALL,
        name="gram",
    )(tokens, *after)


def table_kernel(token_total, chunk, spans_ref, hessian_ref, codes_ref, residue_ref, factor_ref, added_ref, out_ref, sums_ref):
    group = pl.program_id(0)
    width = codes_ref.shape[1]
    tile_count = width // GROUP
    per_chunk = chunk // GROUP
    hessian = hessian_ref[0] / token_total
    high = hessian.astype(jnp.bfloat16)
    high_f = high.astype(jnp.float32)
    low = (hessian - high_f).astype(jnp.bfloat16)
    both = jnp.concatenate([high, low], axis=1)
    half_rows = 0.5 * jnp.sum(high_f + low.astype(jnp.float32), axis=1, keepdims=True)
    sums_ref[...] = jnp.zeros_like(sums_ref)

    def weigh(values):
        return jnp.dot(both, jnp.concatenate([values, values], axis=0), preferred_element_type=jnp.float32)

    def one_chunk(index, carry):
        start = pl.multiple_of(index * chunk, chunk)
        codes = codes_ref[:, pl.ds(start, chunk)]
        rest = residue_ref[:, pl.ds(start, chunk)]
        rest_weighted = weigh(rest) - half_rows
        rest_centred = rest.astype(jnp.float32) - 0.5
        spans = [spans_ref[group, index * per_chunk + t] for t in range(per_chunk)]
        for row, bit_width in enumerate(BIT_WIDTHS[:-1]):
            pieces = []
            for t in range(per_chunk):
                mask = jnp.right_shift(spans[t], bit_width) - 1
                inside = jnp.bitwise_and(codes[:, t * GROUP:(t + 1) * GROUP], mask)
                pieces.append(inside.astype(jnp.float32) - 0.5 * mask.astype(jnp.float32))
            offset = jnp.concatenate(pieces, axis=1)
            weighted = weigh(offset.astype(jnp.bfloat16)) + rest_weighted
            sums_ref[row:row + 1, pl.ds(start, chunk)] = jnp.sum((offset + rest_centred) * weighted, axis=0, keepdims=True)
        last = len(BIT_WIDTHS) - 1
        sums_ref[last:last + 1, pl.ds(start, chunk)] = jnp.sum(rest_centred * rest_weighted, axis=0, keepdims=True)
        return carry

    lax.fori_loop(0, width // chunk, one_chunk, 0)
    lanes = lax.broadcasted_iota(jnp.int32, out_ref.shape[1:], 1)
    totals = jnp.zeros(out_ref.shape[1:], jnp.float32)
    for tile in range(tile_count):
        total = jnp.sum(sums_ref[:, tile * GROUP:(tile + 1) * GROUP], axis=1, keepdims=True)
        totals = jnp.where(lanes == tile, total, totals)
    out_ref[0] = totals * factor_ref[0] + added_ref[0]


def error_table(hessian, grid_codes, residue, tile_spans, tile_scales, token_total):
    group_count, tile_count = tile_spans.shape
    width = grid_codes.shape[1]
    chunk = 256 if width % 256 == 0 else GROUP
    lanes = -(-tile_count // 128) * 128
    bit_count = len(BIT_WIDTHS)
    unit = tile_scales / 128.0
    factor = jnp.broadcast_to((unit * unit / float(GROUP * GROUP))[:, None, :], (group_count, bit_count, tile_count))
    factor = jnp.pad(factor, ((0, 0), (0, 8 - bit_count), (0, lanes - tile_count)))
    added = jnp.stack([tile_spans.astype(jnp.float32), tile_scales], axis=1)
    added = jnp.pad(added, ((0, 0), (bit_count, 6 - bit_count), (0, lanes - tile_count)))
    rows = pl.BlockSpec((1, 8, lanes), lambda g, spans: (g, 0, 0))
    return pl.pallas_call(
        functools.partial(table_kernel, float(token_total), chunk),
        out_shape=jax.ShapeDtypeStruct((group_count, 8, lanes), jnp.float32),
        grid_spec=pltpu.PrefetchScalarGridSpec(
            num_scalar_prefetch=1,
            grid=(group_count,),
            in_specs=[
                pl.BlockSpec((1, GROUP, GROUP), lambda g, spans: (g, 0, 0)),
                pl.BlockSpec((GROUP, width), lambda g, spans: (g, 0)),
                pl.BlockSpec((GROUP, width), lambda g, spans: (g, 0)),
                rows,
                rows,
            ],
            out_specs=rows,
            scratch_shapes=[pltpu.VMEM((8, width), jnp.float32)],
        ),
        compiler_params=params_of(),
        cost_estimate=SMALL,
        name="error_table",
    )(tile_spans, hessian, grid_codes, residue, factor, added)


def probs_of(tables, slope_now):
    scores = [-(ERR_WEIGHT * t + slope_now * float(b)) / SOFTMAX_WARMTH for t, b in zip(tables, BIT_WIDTHS)]
    top = functools.reduce(jnp.maximum, scores)
    raised = [jnp.exp(score - top) for score in scores]
    total = functools.reduce(jnp.add, raised)
    return raised, total


def bits_of(tables, slope_now):
    raised, total = probs_of(tables, slope_now)
    return functools.reduce(jnp.add, [r * float(b) for r, b in zip(raised, BIT_WIDTHS)]) / total


def slope_kernel(tile_count, pack, goal_ref, me_ref, all_ref, coef_ref, bits_ref, tables_ref):
    bit_count = len(BIT_WIDTHS)
    lanes = all_ref.shape[2]
    pitch = lanes // pack
    packed_rows = tables_ref.shape[1]
    for row in range(bit_count):
        packed = all_ref[:packed_rows, row, :]
        for place in range(1, pack):
            part = all_ref[place * packed_rows:(place + 1) * packed_rows, row, :]
            packed = packed + pltpu.roll(part, place * pitch, 1)
        tables_ref[row] = packed
    goal = goal_ref[0]
    lane = lax.broadcasted_iota(jnp.int32, (packed_rows, lanes), 1)
    held = lax.rem(lane, jnp.int32(pitch)) < tile_count

    def trial(index, bounds):
        lower, upper = bounds
        middle = 0.5 * (lower + upper)
        bits = bits_of([tables_ref[row] for row in range(bit_count)], middle)
        above = jnp.sum(jnp.where(held, bits, 0.0)) > goal
        return (jnp.where(above, middle, lower), jnp.where(above, upper, middle))

    lower, upper = lax.fori_loop(0, TRIALS, trial, (jnp.float32(0.0), jnp.float32(SLOPE_LIMIT)))
    slope_final = 0.5 * (lower + upper)

    group_total, _, width = coef_ref.shape
    mine = pl.ds(me_ref[0] * group_total, group_total)
    tables = [all_ref[mine, row, :] for row in range(bit_count)]
    spans, scales = all_ref[mine, bit_count, :], all_ref[mine, bit_count + 1, :]
    bits_ref[...] = bits_of(tables, slope_final)
    raised, total = probs_of(tables, slope_final)
    unit = scales / 128.0
    offset = jnp.zeros_like(unit)
    gains = []
    inverses = []
    for weight, bit_width in zip(raised, BIT_WIDTHS):
        prob = weight / total
        step = jnp.maximum(spans * (0.5 ** bit_width), 1.0)
        gains.append(unit * prob * step)
        inverses.append(1.0 / step)
        offset = offset + 0.5 * unit * prob * step
    rows = [gains[-1], offset] + gains[:-1] + inverses[:-1]
    stacked = jnp.concatenate(rows, axis=0)
    tile = lax.broadcasted_iota(jnp.int32, (lanes, width), 0)
    column = lax.broadcasted_iota(jnp.int32, (lanes, width), 1) + me_ref[1] * width
    first = tile * GROUP
    spread = jnp.where((column >= first) & (column < first + GROUP), 1.0, 0.0)
    columns = jnp.dot(stacked, spread, precision=lax.Precision.HIGHEST, preferred_element_type=jnp.float32)
    for row in range(len(rows)):
        coef_ref[:, row, :] = columns[row * group_total:(row + 1) * group_total]


def find_slope(goal, me, gathered, group_total, tile_count, width):
    group_all, _, lanes = gathered.shape
    pack = 4 if tile_count <= lanes // 4 and group_all % 32 == 0 else 1
    whole = pl.BlockSpec(memory_space=pltpu.VMEM)
    return pl.pallas_call(
        functools.partial(slope_kernel, tile_count, pack),
        out_shape=(
            jax.ShapeDtypeStruct((group_total, 8, width), jnp.float32),
            jax.ShapeDtypeStruct((group_total, lanes), jnp.float32),
        ),
        in_specs=[SCALARS, SCALARS, whole],
        out_specs=(whole, whole),
        scratch_shapes=[pltpu.VMEM((len(BIT_WIDTHS), group_all // pack, lanes), jnp.float32)],
        compiler_params=params_of(),
        cost_estimate=SMALL,
        name="find_slope",
    )(goal.reshape(1), me, gathered)


def serve_kernel(groups, where_ref, codes_ref, coef_ref, *rest):
    out_ref = rest[-1]
    for group in range(groups):
        rows = pl.ds(group * GROUP, GROUP)
        codes = codes_ref[rows, :]
        if codes.dtype == jnp.int32:
            codes = codes - MIDDLE
        codes = codes.astype(jnp.float32)
        mixed = coef_ref[group, 1:2, :] + coef_ref[group, 0:1, :] * codes
        for row in range(len(BIT_WIDTHS) - 1):
            gain = coef_ref[group, 2 + row:3 + row, :]
            inverse = coef_ref[group, 5 + row:6 + row, :]
            mixed = mixed + gain * jnp.floor(codes * inverse)
        out_ref[rows, :] = mixed.astype(jnp.bfloat16)


def serve(codes, column_block, coef, slot, source, rows_each, first_row, row_count, served):
    group_total, _, width = coef.shape
    groups = largest_divisor(row_count // GROUP, 2, 1)
    block = groups * GROUP
    first_block = first_row // block
    steps = rows_each // block
    where = jnp.stack([source, column_block])
    whole_codes = codes.shape[0] != row_count or codes.shape[1] != width
    code_first = first_block if whole_codes else 0
    before = [] if served is None else [served]
    return pl.pallas_call(
        functools.partial(serve_kernel, groups),
        out_shape=jax.ShapeDtypeStruct((group_total * GROUP, width), jnp.bfloat16),
        grid_spec=pltpu.PrefetchScalarGridSpec(
            num_scalar_prefetch=1,
            grid=(row_count // block,),
            in_specs=[
                pl.BlockSpec((block, width), lambda i, where: (code_first + i, where[1])),
                pl.BlockSpec((groups, 8, width), lambda i, where: (slot * steps + first_block + i, 0, 0)),
            ] + [ANY] * len(before),
            out_specs=pl.BlockSpec((block, width), lambda i, where: (where[0] * steps + first_block + i, 0)),
        ),
        input_output_aliases={3: 0} if before else {},
        compiler_params=params_of(),
        cost_estimate=SMALL,
        name="serve",
    )(where, codes, coef, *before)


def local(tokens, grid_codes, residue, tile_spans, tile_scales, other_bits):
    dp_count, mp_count = lax.axis_size("dp"), lax.axis_size("mp")
    me = lax.axis_index("mp").astype(jnp.int32)
    none = jnp.int32(0)
    rows, columns = grid_codes.shape
    width = columns // mp_count
    group_count, tile_count = tile_spans.shape
    group_total = group_count * mp_count
    token_total = tokens.shape[0] * dp_count

    def shifted(value, shift):
        return lax.ppermute(value, "mp", [(z, (z + shift) % mp_count) for z in range(mp_count)])

    def cast(shift, first_row, row_count, after):
        return codes_for(grid_codes, lax.rem(me + shift, mp_count), width, first_row, row_count, after)

    shifts = sorted(range(1, mp_count), key=lambda k: -min(k, mp_count - k))
    loads = [min(k, mp_count - k) for k in shifts]
    early = max(1, sum(1 for i in range(len(shifts)) if 2 * sum(loads[:i]) < sum(loads)))
    whole = [(shift, 0, rows) for shift in shifts]
    first_parts, second_parts = whole[:early], whole[early:]
    half = rows // 2
    if second_parts and group_count % 2 == 0:
        last = second_parts.pop()[0]
        second_parts += [(last, 0, half), (last, half, half)]

    arrived = []
    gram = None
    for part in first_parts:
        sent = cast(*part, [] if gram is None else [gram])
        if gram is None:
            gram = gram_blocks(tokens, [sent])
        arrived.append(shifted(sent, part[0]))

    hessian = lax.psum(gram, "dp")
    table = error_table(hessian, grid_codes, residue, tile_spans, tile_scales, token_total)
    ready = [cast(*part, [table]) for part in second_parts]
    crossing = once_there(table, arrived)
    tables = [table] + [shifted(crossing, shift) for shift in range(1, mp_count)]
    late = []
    for place, (part, sent) in enumerate(zip(second_parts, ready)):
        final = place == len(second_parts) - 1 and place > 1
        after = [late[0]] if final else tables[1:]
        late.append(shifted(once_there(sent, after), part[0]))

    gathered = lax.all_gather(jnp.concatenate(tables), "dp", tiled=True)
    goal = TARGET_BITS * (OTHER + 1) * TILES - jnp.sum(other_bits).astype(jnp.float32)
    places = jnp.stack([lax.axis_index("dp").astype(jnp.int32), me])
    coef, bits = find_slope(goal, places, gathered, group_total, tile_count, width)
    tile_bits = bits[:group_count, :tile_count]

    if width % 128:
        own = cast(0, 0, rows, [])
        served = serve(own, none, coef, 0, me, rows, 0, rows, None)
    else:
        served = serve(grid_codes, me, coef, 0, me, rows, 0, rows, None)
    for (shift, first_row, row_count), codes in zip(first_parts + second_parts, arrived + late):
        source = lax.rem(me + mp_count - shift, mp_count)
        served = serve(codes, none, coef, shift, source, rows, first_row, row_count, served)
    return (served, tile_bits)


def solution(mesh):
    placed = (P("dp", "mp"), P("mp", "dp"), P("mp", "dp"), P("mp", "dp"), P("mp", "dp"), P())
    return jax.shard_map(
        local,
        mesh=mesh,
        in_specs=placed,
        out_specs=(P(None, ("dp", "mp")), P("mp", "dp")),
        check_vma=False,
    )
```

```python
import functools
import math

import jax
import jax.numpy as jnp
from jax import lax
from jax.experimental import pallas as pl
from jax.experimental.pallas import tpu as pltpu
from jax.sharding import PartitionSpec as P

GROUP = 128
TRIALS = 24
OTHER = 8
TILES = 14336


BIT_WIDTHS = (2, 3, 4, 8)
ERR_WEIGHT = 16.0
SOFTMAX_WARMTH = 0.03
SLOPE_LIMIT = 16.0
TARGET_BITS = 3.5
MIDDLE = 128
VMEM_LIMIT = 48 * 1024 * 1024

SMALL = pl.CostEstimate(flops=1000, bytes_accessed=1000, transcendentals=0)
ANY = pl.BlockSpec(memory_space=pl.ANY)
SCALARS = pl.BlockSpec(memory_space=pltpu.SMEM)


def params_of():
    return pltpu.CompilerParams(vmem_limit_bytes=VMEM_LIMIT)


def largest_divisor(total, limit, unit):
    best = unit
    for size in range(unit, limit + 1, unit):
        if total % size == 0:
            best = size
    return best


def touch_kernel(*refs):
    pass


def once_there(value, after):
    return pl.pallas_call(
        touch_kernel,
        out_shape=jax.ShapeDtypeStruct(value.shape, value.dtype),
        in_specs=[ANY] * (1 + len(after)),
        out_specs=ANY,
        input_output_aliases={0: 0},
        compiler_params=params_of(),
        cost_estimate=SMALL,
        name="once_there",
    )(value, *after)


def cast_kernel(reads, where_ref, *refs):
    out_ref = refs[-1]
    for place, codes_ref in enumerate(refs[:reads]):
        block = codes_ref.shape[0]
        centred = (codes_ref[...] - MIDDLE).astype(jnp.float32)
        out_ref[place * block:(place + 1) * block, :] = centred.astype(jnp.bfloat16)


def codes_for(grid_codes, dest, width, first_row, row_count, after):
    if width % 128:
        part = lax.dynamic_slice(grid_codes, (jnp.int32(first_row), dest * width), (row_count, width))
        return (part - MIDDLE).astype(jnp.bfloat16)
    reads = 4
    block = largest_divisor(math.gcd(row_count // reads, first_row), GROUP, GROUP // reads)
    first_block = first_row // block

    def read(place):
        return pl.BlockSpec((block, width), lambda i, where: (first_block + i * reads + place, where[0]))

    return pl.pallas_call(
        functools.partial(cast_kernel, reads),
        out_shape=jax.ShapeDtypeStruct((row_count, width), jnp.bfloat16),
        grid_spec=pltpu.PrefetchScalarGridSpec(
            num_scalar_prefetch=1,
            grid=(row_count // (reads * block),),
            in_specs=[read(place) for place in range(reads)] + [ANY] * len(after),
            out_specs=pl.BlockSpec((reads * block, width), lambda i, where: (i, 0)),
        ),
        compiler_params=params_of(),
        cost_estimate=SMALL,
        name="cast_codes",
    )(dest.reshape(1), *[grid_codes] * reads, *after)


def gram_kernel(tokens_ref, *rest):
    out_ref = rest[-1]
    feats = tokens_ref[...]
    out_ref[0] = lax.dot_general(feats, feats, (((0,), (0,)), ((), ())), preferred_element_type=jnp.float32)


def gram_blocks(tokens, after):
    tok_count, width_local = tokens.shape
    group_count = width_local // GROUP
    return pl.pallas_call(
        gram_kernel,
        out_shape=jax.ShapeDtypeStruct((group_count, GROUP, GROUP), jnp.float32),
        grid=(group_count,),
        in_specs=[pl.BlockSpec((tok_count, GROUP), lambda g: (0, g))] + [ANY] * len(after),
        out_specs=pl.BlockSpec((1, GROUP, GROUP), lambda g: (g, 0, 0)),
        compiler_params=params_of(),
        cost_estimate=SMALL,
        name="gram",
    )(tokens, *after)


def table_kernel(token_total, chunk, pack, spans_ref, hessian_ref, codes_ref, residue_ref, factor_ref, added_ref, out_ref, sums_ref):
    group = pl.program_id(0)
    width = codes_ref.shape[1]
    tile_count = width // GROUP
    per_chunk = chunk // GROUP
    hessian = hessian_ref[0] / token_total
    high = hessian.astype(jnp.bfloat16)
    high_f = high.astype(jnp.float32)
    low = (hessian - high_f).astype(jnp.bfloat16)
    both = jnp.concatenate([high, low], axis=1)
    half_rows = 0.5 * jnp.sum(high_f + low.astype(jnp.float32), axis=1, keepdims=True)
    sums_ref[...] = jnp.zeros_like(sums_ref)

    def weigh(values):
        return jnp.dot(both, jnp.concatenate([values, values], axis=0), preferred_element_type=jnp.float32)

    def one_chunk(index, carry):
        start = pl.multiple_of(index * chunk, chunk)
        codes = codes_ref[:, pl.ds(start, chunk)]
        rest = residue_ref[:, pl.ds(start, chunk)]
        rest_weighted = weigh(rest) - half_rows
        rest_centred = rest.astype(jnp.float32) - 0.5
        spans = [spans_ref[group, index * per_chunk + t] for t in range(per_chunk)]
        for row, bit_width in enumerate(BIT_WIDTHS[:-1]):
            pieces = []
            for t in range(per_chunk):
                mask = jnp.right_shift(spans[t], bit_width) - 1
                inside = jnp.bitwise_and(codes[:, t * GROUP:(t + 1) * GROUP], mask)
                pieces.append(inside.astype(jnp.float32) - 0.5 * mask.astype(jnp.float32))
            offset = jnp.concatenate(pieces, axis=1)
            weighted = weigh(offset.astype(jnp.bfloat16)) + rest_weighted
            sums_ref[row:row + 1, pl.ds(start, chunk)] = jnp.sum((offset + rest_centred) * weighted, axis=0, keepdims=True)
        last = len(BIT_WIDTHS) - 1
        sums_ref[last:last + 1, pl.ds(start, chunk)] = jnp.sum(rest_centred * rest_weighted, axis=0, keepdims=True)
        return carry

    lax.fori_loop(0, width // chunk, one_chunk, 0)
    lanes = lax.broadcasted_iota(jnp.int32, out_ref.shape[1:], 1)
    totals = jnp.zeros(out_ref.shape[1:], jnp.float32)
    for tile in range(tile_count):
        total = jnp.sum(sums_ref[:, tile * GROUP:(tile + 1) * GROUP], axis=1, keepdims=True)
        totals = jnp.where(lanes == tile, total, totals)
    place = lax.rem(group, pack)

    @pl.when(place == 0)
    def _():
        out_ref[...] = jnp.zeros_like(out_ref)

    pitch = out_ref.shape[2] // pack
    out_ref[0] += pltpu.roll(totals * factor_ref[0] + added_ref[0], place * pitch, 1)


def packed_groups(group_count, tile_count):
    return 4 if tile_count <= 32 and group_count % 4 == 0 else 1


def error_table(hessian, grid_codes, residue, tile_spans, tile_scales, token_total):
    group_count, tile_count = tile_spans.shape
    width = grid_codes.shape[1]
    chunk = 256 if width % 256 == 0 else GROUP
    lanes = -(-tile_count // 128) * 128
    pack = packed_groups(group_count, tile_count)
    bit_count = len(BIT_WIDTHS)
    unit = tile_scales / 128.0
    factor = jnp.broadcast_to((unit * unit / float(GROUP * GROUP))[:, None, :], (group_count, bit_count, tile_count))
    factor = jnp.pad(factor, ((0, 0), (0, 8 - bit_count), (0, lanes - tile_count)))
    added = jnp.stack([tile_spans.astype(jnp.float32), tile_scales], axis=1)
    added = jnp.pad(added, ((0, 0), (bit_count, 6 - bit_count), (0, lanes - tile_count)))
    rows = pl.BlockSpec((1, 8, lanes), lambda g, spans: (g, 0, 0))
    return pl.pallas_call(
        functools.partial(table_kernel, float(token_total), chunk, pack),
        out_shape=jax.ShapeDtypeStruct((group_count // pack, 8, lanes), jnp.float32),
        grid_spec=pltpu.PrefetchScalarGridSpec(
            num_scalar_prefetch=1,
            grid=(group_count,),
            in_specs=[
                pl.BlockSpec((1, GROUP, GROUP), lambda g, spans: (g, 0, 0)),
                pl.BlockSpec((GROUP, width), lambda g, spans: (g, 0)),
                pl.BlockSpec((GROUP, width), lambda g, spans: (g, 0)),
                rows,
                rows,
            ],
            out_specs=pl.BlockSpec((1, 8, lanes), lambda g, spans: (g // pack, 0, 0)),
            scratch_shapes=[pltpu.VMEM((8, width), jnp.float32)],
        ),
        compiler_params=params_of(),
        cost_estimate=SMALL,
        name="error_table",
    )(tile_spans, hessian, grid_codes, residue, factor, added)


def probs_of(tables, slope_now):
    scores = [-(ERR_WEIGHT * t + slope_now * float(b)) / SOFTMAX_WARMTH for t, b in zip(tables, BIT_WIDTHS)]
    top = functools.reduce(jnp.maximum, scores)
    raised = [jnp.exp(score - top) for score in scores]
    total = functools.reduce(jnp.add, raised)
    return raised, total


def bits_of(tables, slope_now):
    raised, total = probs_of(tables, slope_now)
    return functools.reduce(jnp.add, [r * float(b) for r, b in zip(raised, BIT_WIDTHS)]) / total


def slope_kernel(tile_count, pack, goal_ref, me_ref, all_ref, coef_ref, bits_ref, tables_ref):
    bit_count = len(BIT_WIDTHS)
    line_count, _, _, lanes = all_ref.shape
    pitch = lanes // pack
    line_rows = bits_ref.shape[0]
    for row in range(bit_count):
        for line in range(line_count):
            tables_ref[row, line * line_rows:(line + 1) * line_rows, :] = all_ref[line, :line_rows, row, :]
    goal = goal_ref[0]
    lane = lax.broadcasted_iota(jnp.int32, tables_ref.shape[1:], 1)
    held = lax.rem(lane, jnp.int32(pitch)) < tile_count

    def trial(index, bounds):
        lower, upper = bounds
        middle = 0.5 * (lower + upper)
        bits = bits_of([tables_ref[row] for row in range(bit_count)], middle)
        above = jnp.sum(jnp.where(held, bits, 0.0)) > goal
        return (jnp.where(above, middle, lower), jnp.where(above, upper, middle))

    lower, upper = lax.fori_loop(0, TRIALS, trial, (jnp.float32(0.0), jnp.float32(SLOPE_LIMIT)))
    slope_final = 0.5 * (lower + upper)

    width = coef_ref.shape[3]
    tables = [all_ref[me_ref[0], :line_rows, row, :] for row in range(bit_count)]
    spans, scales = [all_ref[me_ref[0], :line_rows, row, :] for row in range(bit_count, bit_count + 2)]
    bits_ref[...] = bits_of(tables, slope_final)
    raised, total = probs_of(tables, slope_final)
    unit = scales / 128.0
    offset = jnp.zeros_like(unit)
    gains = []
    inverses = []
    for weight, bit_width in zip(raised, BIT_WIDTHS):
        prob = weight / total
        step = jnp.maximum(spans * (0.5 ** bit_width), 1.0)
        gains.append(unit * prob * step)
        inverses.append(1.0 / step)
        offset = offset + 0.5 * unit * prob * step
    rows = [gains[-1], offset] + gains[:-1] + inverses[:-1]
    stacked = jnp.concatenate(rows, axis=0)
    lane = lax.broadcasted_iota(jnp.int32, (lanes, width), 0)
    column = lax.broadcasted_iota(jnp.int32, (lanes, width), 1) + me_ref[1] * width
    for place in range(pack):
        first = (lane - place * pitch) * GROUP
        spread = jnp.where((column >= first) & (column < first + GROUP), 1.0, 0.0)
        columns = jnp.dot(stacked, spread, precision=lax.Precision.HIGHEST, preferred_element_type=jnp.float32)
        for row in range(len(rows)):
            coef_ref[:, place, row, :] = columns[row * line_rows:(row + 1) * line_rows]


def find_slope(goal, me, gathered, line_rows, pack, tile_count, width):
    line_count, _, _, lanes = gathered.shape
    whole = pl.BlockSpec(memory_space=pltpu.VMEM)
    return pl.pallas_call(
        functools.partial(slope_kernel, tile_count, pack),
        out_shape=(
            jax.ShapeDtypeStruct((line_rows, pack, 8, width), jnp.float32),
            jax.ShapeDtypeStruct((line_rows, lanes), jnp.float32),
        ),
        in_specs=[SCALARS, SCALARS, whole],
        out_specs=(whole, whole),
        scratch_shapes=[pltpu.VMEM((len(BIT_WIDTHS), line_count * line_rows, lanes), jnp.float32)],
        compiler_params=params_of(),
        cost_estimate=SMALL,
        name="find_slope",
    )(goal.reshape(1), me, gathered)


def serve_kernel(groups, where_ref, codes_ref, coef_ref, *rest):
    out_ref = rest[-1]
    width = out_ref.shape[1]
    piece = 32
    for group in range(groups):
        for start in range(0, width, 128):
            lanes = slice(start, min(start + 128, width))
            gain_last, offset = coef_ref[group, 0:1, lanes], coef_ref[group, 1:2, lanes]
            gains = [coef_ref[group, 2 + row:3 + row, lanes] for row in range(len(BIT_WIDTHS) - 1)]
            inverses = [coef_ref[group, 5 + row:6 + row, lanes] for row in range(len(BIT_WIDTHS) - 1)]
            for first in range(group * GROUP, (group + 1) * GROUP, piece):
                rows = slice(first, first + piece)
                codes = codes_ref[rows, lanes]
                if codes.dtype == jnp.int32:
                    codes = codes - MIDDLE
                codes = codes.astype(jnp.float32)
                mixed = offset + gain_last * codes
                for gain, inverse in zip(gains, inverses):
                    mixed = mixed + gain * jnp.floor(codes * inverse)
                out_ref[rows, lanes] = mixed.astype(jnp.bfloat16)


def serve(codes, column_block, coef, slot, source, rows_each, first_row, row_count, served):
    group_total, _, width = coef.shape
    groups = 2 if row_count > 2 * GROUP and row_count % (2 * GROUP) == 0 and first_row % (2 * GROUP) == 0 else 1
    block = groups * GROUP
    first_block = first_row // block
    steps = rows_each // block
    where = jnp.stack([source, column_block])
    whole_codes = codes.shape[0] != row_count or codes.shape[1] != width
    code_first = first_block if whole_codes else 0
    before = [] if served is None else [served]
    return pl.pallas_call(
        functools.partial(serve_kernel, groups),
        out_shape=jax.ShapeDtypeStruct((group_total * GROUP, width), jnp.bfloat16),
        grid_spec=pltpu.PrefetchScalarGridSpec(
            num_scalar_prefetch=1,
            grid=(row_count // block,),
            in_specs=[
                pl.BlockSpec((block, width), lambda i, where: (code_first + i, where[1])),
                pl.BlockSpec((groups, 8, width), lambda i, where: (slot * steps + first_block + i, 0, 0)),
            ] + [ANY] * len(before),
            out_specs=pl.BlockSpec((block, width), lambda i, where: (where[0] * steps + first_block + i, 0)),
        ),
        input_output_aliases={3: 0} if before else {},
        compiler_params=params_of(),
        cost_estimate=SMALL,
        name="serve",
    )(where, codes, coef, *before)


def local(tokens, grid_codes, residue, tile_spans, tile_scales, other_bits):
    dp_count, mp_count = lax.axis_size("dp"), lax.axis_size("mp")
    me = lax.axis_index("mp").astype(jnp.int32)
    none = jnp.int32(0)
    rows, columns = grid_codes.shape
    width = columns // mp_count
    group_count, tile_count = tile_spans.shape
    group_total = group_count * mp_count
    token_total = tokens.shape[0] * dp_count

    def shifted(value, shift):
        return lax.ppermute(value, "mp", [(z, (z + shift) % mp_count) for z in range(mp_count)])

    def cast(shift, first_row, row_count, after):
        return codes_for(grid_codes, lax.rem(me + shift, mp_count), width, first_row, row_count, after)

    shifts = sorted(range(1, mp_count), key=lambda k: -min(k, mp_count - k))
    loads = [min(k, mp_count - k) for k in shifts]
    early = max(1, sum(1 for i in range(len(shifts)) if 2 * sum(loads[:i]) < sum(loads)))
    whole = [(shift, 0, rows) for shift in shifts]
    first_parts, second_parts = whole[:early], whole[early:]
    if group_count % 8 == 0:
        cut = rows // 2
        last = second_parts.pop()[0] if len(second_parts) > 1 else None
        second_parts = [(shift, at, cut) for shift, _, _ in second_parts for at in (0, cut)]
        if last is not None:
            short = rows // 8
            second_parts += [(last, 0, cut), (last, cut, cut - short), (last, rows - short, short)]

    arrived = []
    gram = None
    for part in first_parts:
        sent = cast(*part, [] if gram is None else [gram])
        if gram is None:
            gram = gram_blocks(tokens, [sent])
        arrived.append(shifted(sent, part[0]))

    hessian = lax.psum(gram, "dp")
    table = error_table(hessian, grid_codes, residue, tile_spans, tile_scales, token_total)
    tables = [table] + [shifted(table, shift) for shift in range(1, mp_count)]
    line = jnp.concatenate(tables)
    line_rows = line.shape[0]
    late = []
    for place, part in enumerate(second_parts):
        sent = cast(*part, [table])
        if place == 1:
            sent = once_there(sent, arrived)
        elif place > 1:
            sent = once_there(sent, [late[place - (3 if place == len(second_parts) - 1 and place > 2 else 2)]])
        late.append(shifted(sent, part[0]))

    line = jnp.pad(line, ((0, max(0, 64 - line_rows)), (0, 0), (0, 0)))
    gathered = lax.all_gather(line, "dp")
    goal = TARGET_BITS * (OTHER + 1) * TILES - jnp.sum(other_bits).astype(jnp.float32)
    places = jnp.stack([lax.axis_index("dp").astype(jnp.int32), me])
    pack = packed_groups(group_count, tile_count)
    coef, bits = find_slope(goal, places, gathered, line_rows, pack, tile_count, width)
    coef = coef.reshape(group_total, 8, width)
    tile_bits = bits[:group_count // pack].reshape(group_count, -1)[:, :tile_count]

    if width % 128:
        own = cast(0, 0, rows, [])
        served = serve(own, none, coef, 0, me, rows, 0, rows, None)
    else:
        served = serve(grid_codes, me, coef, 0, me, rows, 0, rows, None)
    for (shift, first_row, row_count), codes in zip(first_parts + second_parts, arrived + late):
        source = lax.rem(me + mp_count - shift, mp_count)
        served = serve(codes, none, coef, shift, source, rows, first_row, row_count, served)
    return (served, tile_bits)


def solution(mesh):
    placed = (P("dp", "mp"), P("mp", "dp"), P("mp", "dp"), P("mp", "dp"), P("mp", "dp"), P())
    return jax.shard_map(
        local,
        mesh=mesh,
        in_specs=placed,
        out_specs=(P(None, ("dp", "mp")), P("mp", "dp")),
        check_vma=False,
    )
```

```python
import functools
import math

import jax
import jax.numpy as jnp
from jax import lax
from jax.experimental import pallas as pl
from jax.experimental.pallas import tpu as pltpu
from jax.sharding import PartitionSpec as P

GROUP = 128
TRIALS = 24
OTHER = 8
TILES = 14336


BIT_WIDTHS = (2, 3, 4, 8)
ERR_WEIGHT = 16.0
SOFTMAX_WARMTH = 0.03
SLOPE_LIMIT = 16.0
TARGET_BITS = 3.5
MIDDLE = 127.5
ROUNDER = 1.5 * 2.0 ** 23
VMEM_LIMIT = 48 * 1024 * 1024

SMALL = pl.CostEstimate(flops=1000, bytes_accessed=1000, transcendentals=0)
ANY = pl.BlockSpec(memory_space=pl.ANY)
SCALARS = pl.BlockSpec(memory_space=pltpu.SMEM)


def params_of():
    return pltpu.CompilerParams(vmem_limit_bytes=VMEM_LIMIT)


def largest_divisor(total, limit, unit):
    best = unit
    for size in range(unit, limit + 1, unit):
        if total % size == 0:
            best = size
    return best


def touch_kernel(*refs):
    pass


def once_there(value, after):
    return pl.pallas_call(
        touch_kernel,
        out_shape=jax.ShapeDtypeStruct(value.shape, value.dtype),
        in_specs=[ANY] * (1 + len(after)),
        out_specs=ANY,
        input_output_aliases={0: 0},
        compiler_params=params_of(),
        cost_estimate=SMALL,
        name="once_there",
    )(value, *after)


def cast_kernel(reads, where_ref, *refs):
    out_ref = refs[-1]
    for place, codes_ref in enumerate(refs[:reads]):
        block = codes_ref.shape[0]
        centred = codes_ref[...].astype(jnp.float32) - MIDDLE
        out_ref[place * block:(place + 1) * block, :] = centred.astype(jnp.bfloat16)


def codes_for(grid_codes, dest, width, first_row, row_count, after):
    if width % 128:
        part = lax.dynamic_slice(grid_codes, (jnp.int32(first_row), dest * width), (row_count, width))
        return (part.astype(jnp.float32) - MIDDLE).astype(jnp.bfloat16)
    reads = 4
    block = largest_divisor(math.gcd(row_count // reads, first_row), GROUP, GROUP // reads)
    first_block = first_row // block

    def read(place):
        return pl.BlockSpec((block, width), lambda i, where: (first_block + i * reads + place, where[0]))

    return pl.pallas_call(
        functools.partial(cast_kernel, reads),
        out_shape=jax.ShapeDtypeStruct((row_count, width), jnp.bfloat16),
        grid_spec=pltpu.PrefetchScalarGridSpec(
            num_scalar_prefetch=1,
            grid=(row_count // (reads * block),),
            in_specs=[read(place) for place in range(reads)] + [ANY] * len(after),
            out_specs=pl.BlockSpec((reads * block, width), lambda i, where: (i, 0)),
        ),
        compiler_params=params_of(),
        cost_estimate=SMALL,
        name="cast_codes",
    )(dest.reshape(1), *[grid_codes] * reads, *after)


def gram_kernel(tokens_ref, *rest):
    out_ref = rest[-1]
    feats = tokens_ref[...]
    out_ref[0] = lax.dot_general(feats, feats, (((0,), (0,)), ((), ())), preferred_element_type=jnp.float32)


def gram_blocks(tokens, after):
    tok_count, width_local = tokens.shape
    group_count = width_local // GROUP
    return pl.pallas_call(
        gram_kernel,
        out_shape=jax.ShapeDtypeStruct((group_count, GROUP, GROUP), jnp.float32),
        grid=(group_count,),
        in_specs=[pl.BlockSpec((tok_count, GROUP), lambda g: (0, g))] + [ANY] * len(after),
        out_specs=pl.BlockSpec((1, GROUP, GROUP), lambda g: (g, 0, 0)),
        compiler_params=params_of(),
        cost_estimate=SMALL,
        name="gram",
    )(tokens, *after)


def table_kernel(token_total, chunk, pack, spans_ref, hessian_ref, codes_ref, residue_ref, factor_ref, added_ref, out_ref, sums_ref):
    group = pl.program_id(0)
    width = codes_ref.shape[1]
    tile_count = width // GROUP
    per_chunk = chunk // GROUP
    hessian = hessian_ref[0] / token_total
    high = hessian.astype(jnp.bfloat16)
    high_f = high.astype(jnp.float32)
    low = (hessian - high_f).astype(jnp.bfloat16)
    both = jnp.concatenate([high, low], axis=1)
    half_rows = 0.5 * jnp.sum(high_f + low.astype(jnp.float32), axis=1, keepdims=True)
    sums_ref[...] = jnp.zeros_like(sums_ref)

    def weigh(values):
        return jnp.dot(both, jnp.concatenate([values, values], axis=0), preferred_element_type=jnp.float32)

    def one_chunk(index, carry):
        start = pl.multiple_of(index * chunk, chunk)
        codes = codes_ref[:, pl.ds(start, chunk)]
        rest = residue_ref[:, pl.ds(start, chunk)]
        rest_weighted = weigh(rest) - half_rows
        rest_centred = rest.astype(jnp.float32) - 0.5
        spans = [spans_ref[group, index * per_chunk + t] for t in range(per_chunk)]
        for row, bit_width in enumerate(BIT_WIDTHS[:-1]):
            pieces = []
            for t in range(per_chunk):
                mask = jnp.right_shift(spans[t], bit_width) - 1
                inside = jnp.bitwise_and(codes[:, t * GROUP:(t + 1) * GROUP], mask)
                pieces.append(inside.astype(jnp.float32) - 0.5 * mask.astype(jnp.float32))
            offset = jnp.concatenate(pieces, axis=1)
            weighted = weigh(offset.astype(jnp.bfloat16)) + rest_weighted
            sums_ref[row:row + 1, pl.ds(start, chunk)] = jnp.sum((offset + rest_centred) * weighted, axis=0, keepdims=True)
        last = len(BIT_WIDTHS) - 1
        sums_ref[last:last + 1, pl.ds(start, chunk)] = jnp.sum(rest_centred * rest_weighted, axis=0, keepdims=True)
        return carry

    lax.fori_loop(0, width // chunk, one_chunk, 0)
    lanes = lax.broadcasted_iota(jnp.int32, out_ref.shape[1:], 1)
    totals = jnp.zeros(out_ref.shape[1:], jnp.float32)
    for tile in range(tile_count):
        total = jnp.sum(sums_ref[:, tile * GROUP:(tile + 1) * GROUP], axis=1, keepdims=True)
        totals = jnp.where(lanes == tile, total, totals)
    place = lax.rem(group, pack)

    @pl.when(place == 0)
    def _():
        out_ref[...] = jnp.zeros_like(out_ref)

    pitch = out_ref.shape[2] // pack
    out_ref[0] += pltpu.roll(totals * factor_ref[0] + added_ref[0], place * pitch, 1)


def packed_groups(group_count, tile_count):
    return 4 if tile_count <= 32 and group_count % 4 == 0 else 1


def error_table(hessian, grid_codes, residue, tile_spans, tile_scales, token_total):
    group_count, tile_count = tile_spans.shape
    width = grid_codes.shape[1]
    chunk = 256 if width % 256 == 0 else GROUP
    lanes = -(-tile_count // 128) * 128
    pack = packed_groups(group_count, tile_count)
    bit_count = len(BIT_WIDTHS)
    unit = tile_scales / 128.0
    factor = jnp.broadcast_to((unit * unit / float(GROUP * GROUP))[:, None, :], (group_count, bit_count, tile_count))
    factor = jnp.pad(factor, ((0, 0), (0, 8 - bit_count), (0, lanes - tile_count)))
    added = jnp.stack([tile_spans.astype(jnp.float32), tile_scales], axis=1)
    added = jnp.pad(added, ((0, 0), (bit_count, 6 - bit_count), (0, lanes - tile_count)))
    rows = pl.BlockSpec((1, 8, lanes), lambda g, spans: (g, 0, 0))
    return pl.pallas_call(
        functools.partial(table_kernel, float(token_total), chunk, pack),
        out_shape=jax.ShapeDtypeStruct((group_count // pack, 8, lanes), jnp.float32),
        grid_spec=pltpu.PrefetchScalarGridSpec(
            num_scalar_prefetch=1,
            grid=(group_count,),
            in_specs=[
                pl.BlockSpec((1, GROUP, GROUP), lambda g, spans: (g, 0, 0)),
                pl.BlockSpec((GROUP, width), lambda g, spans: (g, 0)),
                pl.BlockSpec((GROUP, width), lambda g, spans: (g, 0)),
                rows,
                rows,
            ],
            out_specs=pl.BlockSpec((1, 8, lanes), lambda g, spans: (g // pack, 0, 0)),
            scratch_shapes=[pltpu.VMEM((8, width), jnp.float32)],
        ),
        compiler_params=params_of(),
        cost_estimate=SMALL,
        name="error_table",
    )(tile_spans, hessian, grid_codes, residue, factor, added)


def probs_of(tables, slope_now):
    scores = [-(ERR_WEIGHT * t + slope_now * float(b)) / SOFTMAX_WARMTH for t, b in zip(tables, BIT_WIDTHS)]
    top = functools.reduce(jnp.maximum, scores)
    raised = [jnp.exp(score - top) for score in scores]
    total = functools.reduce(jnp.add, raised)
    return raised, total


def bits_of(tables, slope_now):
    raised, total = probs_of(tables, slope_now)
    return functools.reduce(jnp.add, [r * float(b) for r, b in zip(raised, BIT_WIDTHS)]) / total


def slope_kernel(tile_count, pack, goal_ref, me_ref, all_ref, coef_ref, bits_ref, tables_ref):
    bit_count = len(BIT_WIDTHS)
    line_count, _, _, lanes = all_ref.shape
    pitch = lanes // pack
    line_rows = bits_ref.shape[0]
    for row in range(bit_count):
        for line in range(line_count):
            tables_ref[row, line * line_rows:(line + 1) * line_rows, :] = all_ref[line, :line_rows, row, :]
    goal = goal_ref[0]
    lane = lax.broadcasted_iota(jnp.int32, tables_ref.shape[1:], 1)
    held = lax.rem(lane, jnp.int32(pitch)) < tile_count

    def trial(index, bounds):
        lower, upper = bounds
        middle = 0.5 * (lower + upper)
        bits = bits_of([tables_ref[row] for row in range(bit_count)], middle)
        above = jnp.sum(jnp.where(held, bits, 0.0)) > goal
        return (jnp.where(above, middle, lower), jnp.where(above, upper, middle))

    lower, upper = lax.fori_loop(0, TRIALS, trial, (jnp.float32(0.0), jnp.float32(SLOPE_LIMIT)))
    slope_final = 0.5 * (lower + upper)

    width = coef_ref.shape[3]
    tables = [all_ref[me_ref[0], :line_rows, row, :] for row in range(bit_count)]
    spans, scales = [all_ref[me_ref[0], :line_rows, row, :] for row in range(bit_count, bit_count + 2)]
    bits_ref[...] = bits_of(tables, slope_final)
    raised, total = probs_of(tables, slope_final)
    unit = scales / 128.0
    offset = jnp.zeros_like(unit)
    gains = []
    steps = []
    for weight, bit_width in zip(raised[:-1], BIT_WIDTHS):
        step = jnp.maximum(spans * (0.5 ** bit_width), 1.0)
        gains.append(unit * (weight / total))
        steps.append(step)
        offset = offset + gains[-1] * (0.5 * step)
    rows = [unit * (raised[-1] / total), offset] + gains + steps
    stacked = jnp.concatenate(rows, axis=0)
    lane = lax.broadcasted_iota(jnp.int32, (lanes, width), 0)
    column = lax.broadcasted_iota(jnp.int32, (lanes, width), 1) + me_ref[1] * width
    for place in range(pack):
        first = (lane - place * pitch) * GROUP
        spread = jnp.where((column >= first) & (column < first + GROUP), 1.0, 0.0)
        columns = jnp.dot(stacked, spread, precision=lax.Precision.HIGHEST, preferred_element_type=jnp.float32)
        for row in range(len(rows)):
            coef_ref[:, place, row, :] = columns[row * line_rows:(row + 1) * line_rows]


def find_slope(goal, me, gathered, line_rows, pack, tile_count, width):
    line_count, _, _, lanes = gathered.shape
    whole = pl.BlockSpec(memory_space=pltpu.VMEM)
    return pl.pallas_call(
        functools.partial(slope_kernel, tile_count, pack),
        out_shape=(
            jax.ShapeDtypeStruct((line_rows, pack, 8, width), jnp.float32),
            jax.ShapeDtypeStruct((line_rows, lanes), jnp.float32),
        ),
        in_specs=[SCALARS, SCALARS, whole],
        out_specs=(whole, whole),
        scratch_shapes=[pltpu.VMEM((len(BIT_WIDTHS), line_count * line_rows, lanes), jnp.float32)],
        compiler_params=params_of(),
        cost_estimate=SMALL,
        name="find_slope",
    )(goal.reshape(1), me, gathered)


def serve_kernel(groups, where_ref, codes_ref, coef_ref, *rest):
    out_ref = rest[-1]
    width = out_ref.shape[1]
    piece = 32
    for group in range(groups):
        for start in range(0, width, 128):
            lanes = slice(start, min(start + 128, width))
            gain_last, offset = coef_ref[group, 0:1, lanes], coef_ref[group, 1:2, lanes]
            gains = [coef_ref[group, 2 + row:3 + row, lanes] for row in range(len(BIT_WIDTHS) - 1)]
            steps = [coef_ref[group, 5 + row:6 + row, lanes] for row in range(len(BIT_WIDTHS) - 1)]
            halves = [0.5 * step for step in steps]
            rounders = [ROUNDER * step for step in steps]
            for first in range(group * GROUP, (group + 1) * GROUP, piece):
                rows = slice(first, first + piece)
                codes = codes_ref[rows, lanes].astype(jnp.float32)
                if codes_ref.dtype == jnp.int32:
                    codes = codes - MIDDLE
                mixed = offset + gain_last * codes
                for gain, half, rounder in zip(gains, halves, rounders):
                    mixed = mixed + gain * (((codes - half) + rounder) - rounder)
                out_ref[rows, lanes] = mixed.astype(jnp.bfloat16)


def serve(codes, column_block, coef, slot, source, rows_each, first_row, row_count, served):
    group_total, _, width = coef.shape
    groups = 2 if row_count > 2 * GROUP and row_count % (2 * GROUP) == 0 and first_row % (2 * GROUP) == 0 else 1
    block = groups * GROUP
    first_block = first_row // block
    steps = rows_each // block
    where = jnp.stack([source, column_block])
    whole_codes = codes.shape[0] != row_count or codes.shape[1] != width
    code_first = first_block if whole_codes else 0
    before = [] if served is None else [served]
    return pl.pallas_call(
        functools.partial(serve_kernel, groups),
        out_shape=jax.ShapeDtypeStruct((group_total * GROUP, width), jnp.bfloat16),
        grid_spec=pltpu.PrefetchScalarGridSpec(
            num_scalar_prefetch=1,
            grid=(row_count // block,),
            in_specs=[
                pl.BlockSpec((block, width), lambda i, where: (code_first + i, where[1])),
                pl.BlockSpec((groups, 8, width), lambda i, where: (slot * steps + first_block + i, 0, 0)),
            ] + [ANY] * len(before),
            out_specs=pl.BlockSpec((block, width), lambda i, where: (where[0] * steps + first_block + i, 0)),
        ),
        input_output_aliases={3: 0} if before else {},
        compiler_params=params_of(),
        cost_estimate=SMALL,
        name="serve",
    )(where, codes, coef, *before)


def local(tokens, grid_codes, residue, tile_spans, tile_scales, other_bits):
    dp_count, mp_count = lax.axis_size("dp"), lax.axis_size("mp")
    me = lax.axis_index("mp").astype(jnp.int32)
    none = jnp.int32(0)
    rows, columns = grid_codes.shape
    width = columns // mp_count
    group_count, tile_count = tile_spans.shape
    group_total = group_count * mp_count
    token_total = tokens.shape[0] * dp_count

    def shifted(value, shift):
        return lax.ppermute(value, "mp", [(z, (z + shift) % mp_count) for z in range(mp_count)])

    def cast(shift, first_row, row_count, after):
        return codes_for(grid_codes, lax.rem(me + shift, mp_count), width, first_row, row_count, after)

    shifts = sorted(range(1, mp_count), key=lambda k: -min(k, mp_count - k))
    loads = [min(k, mp_count - k) for k in shifts]
    early = max(1, sum(1 for i in range(len(shifts)) if 2 * sum(loads[:i]) < sum(loads)))
    whole = [(shift, 0, rows) for shift in shifts]
    first_parts, second_parts = whole[:early], whole[early:]
    if group_count % 8 == 0 and len(second_parts) > 1:
        last = second_parts.pop()[0]
        cut, short = rows // 2, rows // 8
        second_parts += [(last, 0, cut), (last, cut, cut - short), (last, rows - short, short)]

    arrived = []
    gram = None
    for part in first_parts:
        sent = cast(*part, [] if gram is None else [gram])
        if gram is None:
            gram = gram_blocks(tokens, [sent])
        arrived.append(shifted(sent, part[0]))

    hessian = lax.psum(gram, "dp")
    table = error_table(hessian, grid_codes, residue, tile_spans, tile_scales, token_total)
    ready = [cast(*part, [table]) for part in second_parts]
    crossing = once_there(table, ready[:1])
    tables = [table] + [shifted(crossing, shift) for shift in range(1, mp_count)]
    line = once_there(jnp.concatenate(tables), arrived)
    line_rows = line.shape[0]
    late = []
    for place, (part, sent) in enumerate(zip(second_parts, ready)):
        if place == 1:
            sent = once_there(sent, arrived)
        elif place > 1:
            sent = once_there(sent, [late[0]])
        late.append(shifted(sent, part[0]))

    line = jnp.pad(line, ((0, max(0, 64 - line_rows)), (0, 0), (0, 0)))
    gathered = lax.all_gather(line, "dp")
    goal = TARGET_BITS * (OTHER + 1) * TILES - jnp.sum(other_bits).astype(jnp.float32)
    places = jnp.stack([lax.axis_index("dp").astype(jnp.int32), me])
    pack = packed_groups(group_count, tile_count)
    coef, bits = find_slope(goal, places, gathered, line_rows, pack, tile_count, width)
    coef = coef.reshape(group_total, 8, width)
    tile_bits = bits[:group_count // pack].reshape(group_count, -1)[:, :tile_count]

    if width % 128:
        own = cast(0, 0, rows, [])
        served = serve(own, none, coef, 0, me, rows, 0, rows, None)
    else:
        served = serve(grid_codes, me, coef, 0, me, rows, 0, rows, None)
    for (shift, first_row, row_count), codes in zip(first_parts + second_parts, arrived + late):
        source = lax.rem(me + mp_count - shift, mp_count)
        served = serve(codes, none, coef, shift, source, rows, first_row, row_count, served)
    return (served, tile_bits)


def solution(mesh):
    placed = (P("dp", "mp"), P("mp", "dp"), P("mp", "dp"), P("mp", "dp"), P("mp", "dp"), P())
    return jax.shard_map(
        local,
        mesh=mesh,
        in_specs=placed,
        out_specs=(P(None, ("dp", "mp")), P("mp", "dp")),
        check_vma=False,
    )
```

```python
import functools
import math

import jax
import jax.numpy as jnp
from jax import lax
from jax.experimental import pallas as pl
from jax.experimental.pallas import tpu as pltpu
from jax.sharding import PartitionSpec as P

GROUP = 128
TRIALS = 24
OTHER = 8
TILES = 14336


BIT_WIDTHS = (2, 3, 4, 8)
ERR_WEIGHT = 16.0
SOFTMAX_WARMTH = 0.03
SLOPE_LIMIT = 16.0
TARGET_BITS = 3.5
MIDDLE = 127.5
ROUNDER = 1.5 * 2.0 ** 23
VMEM_LIMIT = 48 * 1024 * 1024

SMALL = pl.CostEstimate(flops=1000, bytes_accessed=1000, transcendentals=0)
ANY = pl.BlockSpec(memory_space=pl.ANY)
SCALARS = pl.BlockSpec(memory_space=pltpu.SMEM)


def params_of():
    return pltpu.CompilerParams(vmem_limit_bytes=VMEM_LIMIT)


def largest_divisor(total, limit, unit):
    best = unit
    for size in range(unit, limit + 1, unit):
        if total % size == 0:
            best = size
    return best


def touch_kernel(*refs):
    pass


def once_there(value, after):
    return pl.pallas_call(
        touch_kernel,
        out_shape=jax.ShapeDtypeStruct(value.shape, value.dtype),
        in_specs=[ANY] * (1 + len(after)),
        out_specs=ANY,
        input_output_aliases={0: 0},
        compiler_params=params_of(),
        cost_estimate=SMALL,
        name="once_there",
    )(value, *after)


def cast_kernel(reads, where_ref, *refs):
    out_ref = refs[-1]
    for place, codes_ref in enumerate(refs[:reads]):
        block = codes_ref.shape[0]
        centred = codes_ref[...].astype(jnp.float32) - MIDDLE
        out_ref[place * block:(place + 1) * block, :] = centred.astype(jnp.bfloat16)


def codes_for(grid_codes, dest, width, first_row, row_count, after):
    if width % 128:
        part = lax.dynamic_slice(grid_codes, (jnp.int32(first_row), dest * width), (row_count, width))
        return (part.astype(jnp.float32) - MIDDLE).astype(jnp.bfloat16)
    reads = 4
    block = largest_divisor(math.gcd(row_count // reads, first_row), GROUP, GROUP // reads)
    first_block = first_row // block

    def read(place):
        return pl.BlockSpec((block, width), lambda i, where: (first_block + i * reads + place, where[0]))

    return pl.pallas_call(
        functools.partial(cast_kernel, reads),
        out_shape=jax.ShapeDtypeStruct((row_count, width), jnp.bfloat16),
        grid_spec=pltpu.PrefetchScalarGridSpec(
            num_scalar_prefetch=1,
            grid=(row_count // (reads * block),),
            in_specs=[read(place) for place in range(reads)] + [ANY] * len(after),
            out_specs=pl.BlockSpec((reads * block, width), lambda i, where: (i, 0)),
        ),
        compiler_params=params_of(),
        cost_estimate=SMALL,
        name="cast_codes",
    )(dest.reshape(1), *[grid_codes] * reads, *after)


def gram_kernel(tokens_ref, *rest):
    out_ref = rest[-1]
    feats = tokens_ref[...]
    out_ref[0] = lax.dot_general(feats, feats, (((0,), (0,)), ((), ())), preferred_element_type=jnp.float32)


def gram_blocks(tokens, after):
    tok_count, width_local = tokens.shape
    group_count = width_local // GROUP
    return pl.pallas_call(
        gram_kernel,
        out_shape=jax.ShapeDtypeStruct((group_count, GROUP, GROUP), jnp.float32),
        grid=(group_count,),
        in_specs=[pl.BlockSpec((tok_count, GROUP), lambda g: (0, g))] + [ANY] * len(after),
        out_specs=pl.BlockSpec((1, GROUP, GROUP), lambda g: (g, 0, 0)),
        compiler_params=params_of(),
        cost_estimate=SMALL,
        name="gram",
    )(tokens, *after)


def table_kernel(token_total, chunk, pack, spans_ref, hessian_ref, codes_ref, residue_ref, factor_ref, added_ref, out_ref, sums_ref):
    group = pl.program_id(0)
    width = codes_ref.shape[1]
    tile_count = width // GROUP
    per_chunk = chunk // GROUP
    hessian = hessian_ref[0] / token_total
    high = hessian.astype(jnp.bfloat16)
    high_f = high.astype(jnp.float32)
    low = (hessian - high_f).astype(jnp.bfloat16)
    both = jnp.concatenate([high, low], axis=1)
    half_rows = 0.5 * jnp.sum(high_f + low.astype(jnp.float32), axis=1, keepdims=True)
    sums_ref[...] = jnp.zeros_like(sums_ref)

    def weigh(values):
        return jnp.dot(both, jnp.concatenate([values, values], axis=0), preferred_element_type=jnp.float32)

    def one_chunk(index, carry):
        start = pl.multiple_of(index * chunk, chunk)
        codes = codes_ref[:, pl.ds(start, chunk)]
        rest = residue_ref[:, pl.ds(start, chunk)]
        rest_weighted = weigh(rest) - half_rows
        rest_centred = rest.astype(jnp.float32) - 0.5
        spans = [spans_ref[group, index * per_chunk + t] for t in range(per_chunk)]
        for row, bit_width in enumerate(BIT_WIDTHS[:-1]):
            pieces = []
            for t in range(per_chunk):
                mask = jnp.right_shift(spans[t], bit_width) - 1
                inside = jnp.bitwise_and(codes[:, t * GROUP:(t + 1) * GROUP], mask)
                pieces.append(inside.astype(jnp.float32) - 0.5 * mask.astype(jnp.float32))
            offset = jnp.concatenate(pieces, axis=1)
            weighted = weigh(offset.astype(jnp.bfloat16)) + rest_weighted
            sums_ref[row:row + 1, pl.ds(start, chunk)] = jnp.sum((offset + rest_centred) * weighted, axis=0, keepdims=True)
        last = len(BIT_WIDTHS) - 1
        sums_ref[last:last + 1, pl.ds(start, chunk)] = jnp.sum(rest_centred * rest_weighted, axis=0, keepdims=True)
        return carry

    lax.fori_loop(0, width // chunk, one_chunk, 0)
    lanes = lax.broadcasted_iota(jnp.int32, out_ref.shape[1:], 1)
    totals = jnp.zeros(out_ref.shape[1:], jnp.float32)
    for tile in range(tile_count):
        total = jnp.sum(sums_ref[:, tile * GROUP:(tile + 1) * GROUP], axis=1, keepdims=True)
        totals = jnp.where(lanes == tile, total, totals)
    place = lax.rem(group, pack)

    @pl.when(place == 0)
    def _():
        out_ref[...] = jnp.zeros_like(out_ref)

    pitch = out_ref.shape[2] // pack
    out_ref[0] += pltpu.roll(totals * factor_ref[0] + added_ref[0], place * pitch, 1)


def packed_groups(group_count, tile_count):
    return 4 if tile_count <= 32 and group_count % 4 == 0 else 1


def error_table(hessian, grid_codes, residue, tile_spans, tile_scales, token_total):
    group_count, tile_count = tile_spans.shape
    width = grid_codes.shape[1]
    chunk = 256 if width % 256 == 0 else GROUP
    lanes = -(-tile_count // 128) * 128
    pack = packed_groups(group_count, tile_count)
    bit_count = len(BIT_WIDTHS)
    unit = tile_scales / 128.0
    factor = jnp.broadcast_to((unit * unit / float(GROUP * GROUP))[:, None, :], (group_count, bit_count, tile_count))
    factor = jnp.pad(factor, ((0, 0), (0, 8 - bit_count), (0, lanes - tile_count)))
    added = jnp.stack([tile_spans.astype(jnp.float32), tile_scales], axis=1)
    added = jnp.pad(added, ((0, 0), (bit_count, 6 - bit_count), (0, lanes - tile_count)))
    rows = pl.BlockSpec((1, 8, lanes), lambda g, spans: (g, 0, 0))
    return pl.pallas_call(
        functools.partial(table_kernel, float(token_total), chunk, pack),
        out_shape=jax.ShapeDtypeStruct((group_count // pack, 8, lanes), jnp.float32),
        grid_spec=pltpu.PrefetchScalarGridSpec(
            num_scalar_prefetch=1,
            grid=(group_count,),
            in_specs=[
                pl.BlockSpec((1, GROUP, GROUP), lambda g, spans: (g, 0, 0)),
                pl.BlockSpec((GROUP, width), lambda g, spans: (g, 0)),
                pl.BlockSpec((GROUP, width), lambda g, spans: (g, 0)),
                rows,
                rows,
            ],
            out_specs=pl.BlockSpec((1, 8, lanes), lambda g, spans: (g // pack, 0, 0)),
            scratch_shapes=[pltpu.VMEM((8, width), jnp.float32)],
        ),
        compiler_params=params_of(),
        cost_estimate=SMALL,
        name="error_table",
    )(tile_spans, hessian, grid_codes, residue, factor, added)


def probs_of(tables, slope_now):
    scores = [-(ERR_WEIGHT * t + slope_now * float(b)) / SOFTMAX_WARMTH for t, b in zip(tables, BIT_WIDTHS)]
    top = functools.reduce(jnp.maximum, scores)
    raised = [jnp.exp(score - top) for score in scores]
    total = functools.reduce(jnp.add, raised)
    return raised, total


def bits_of(tables, slope_now):
    raised, total = probs_of(tables, slope_now)
    return functools.reduce(jnp.add, [r * float(b) for r, b in zip(raised, BIT_WIDTHS)]) / total


def slope_kernel(tile_count, pack, goal_ref, me_ref, all_ref, coef_ref, bits_ref, tables_ref):
    bit_count = len(BIT_WIDTHS)
    line_count, _, _, lanes = all_ref.shape
    pitch = lanes // pack
    line_rows = bits_ref.shape[0]
    for row in range(bit_count):
        for line in range(line_count):
            tables_ref[row, line * line_rows:(line + 1) * line_rows, :] = all_ref[line, :line_rows, row, :]
    goal = goal_ref[0]
    lane = lax.broadcasted_iota(jnp.int32, tables_ref.shape[1:], 1)
    held = lax.rem(lane, jnp.int32(pitch)) < tile_count

    def trial(index, bounds):
        lower, upper = bounds
        middle = 0.5 * (lower + upper)
        bits = bits_of([tables_ref[row] for row in range(bit_count)], middle)
        above = jnp.sum(jnp.where(held, bits, 0.0)) > goal
        return (jnp.where(above, middle, lower), jnp.where(above, upper, middle))

    lower, upper = lax.fori_loop(0, TRIALS, trial, (jnp.float32(0.0), jnp.float32(SLOPE_LIMIT)))
    slope_final = 0.5 * (lower + upper)

    width = coef_ref.shape[3]
    tables = [all_ref[me_ref[0], :line_rows, row, :] for row in range(bit_count)]
    spans, scales = [all_ref[me_ref[0], :line_rows, row, :] for row in range(bit_count, bit_count + 2)]
    bits_ref[...] = bits_of(tables, slope_final)
    raised, total = probs_of(tables, slope_final)
    unit = scales / 128.0
    offset = jnp.zeros_like(unit)
    gains = []
    steps = []
    for weight, bit_width in zip(raised[:-1], BIT_WIDTHS):
        step = jnp.maximum(spans * (0.5 ** bit_width), 1.0)
        gains.append(unit * (weight / total))
        steps.append(step)
        offset = offset + gains[-1] * (0.5 * step)
    rows = [unit * (raised[-1] / total), offset] + gains + steps
    stacked = jnp.concatenate(rows, axis=0)
    lane = lax.broadcasted_iota(jnp.int32, (lanes, width), 0)
    column = lax.broadcasted_iota(jnp.int32, (lanes, width), 1) + me_ref[1] * width
    for place in range(pack):
        first = (lane - place * pitch) * GROUP
        spread = jnp.where((column >= first) & (column < first + GROUP), 1.0, 0.0)
        columns = jnp.dot(stacked, spread, precision=lax.Precision.HIGHEST, preferred_element_type=jnp.float32)
        for row in range(len(rows)):
            coef_ref[:, place, row, :] = columns[row * line_rows:(row + 1) * line_rows]


def find_slope(goal, me, gathered, line_rows, pack, tile_count, width):
    line_count, _, _, lanes = gathered.shape
    whole = pl.BlockSpec(memory_space=pltpu.VMEM)
    return pl.pallas_call(
        functools.partial(slope_kernel, tile_count, pack),
        out_shape=(
            jax.ShapeDtypeStruct((line_rows, pack, 8, width), jnp.float32),
            jax.ShapeDtypeStruct((line_rows, lanes), jnp.float32),
        ),
        in_specs=[SCALARS, SCALARS, whole],
        out_specs=(whole, whole),
        scratch_shapes=[pltpu.VMEM((len(BIT_WIDTHS), line_count * line_rows, lanes), jnp.float32)],
        compiler_params=params_of(),
        cost_estimate=SMALL,
        name="find_slope",
    )(goal.reshape(1), me, gathered)


def serve_kernel(groups, where_ref, codes_ref, coef_ref, *rest):
    out_ref = rest[-1]
    width = out_ref.shape[1]
    piece = 32
    for group in range(groups):
        for start in range(0, width, 128):
            lanes = slice(start, min(start + 128, width))
            gain_last, offset = coef_ref[group, 0:1, lanes], coef_ref[group, 1:2, lanes]
            gains = [coef_ref[group, 2 + row:3 + row, lanes] for row in range(len(BIT_WIDTHS) - 1)]
            steps = [coef_ref[group, 5 + row:6 + row, lanes] for row in range(len(BIT_WIDTHS) - 1)]
            halves = [0.5 * step for step in steps]
            rounders = [ROUNDER * step for step in steps]
            for first in range(group * GROUP, (group + 1) * GROUP, piece):
                rows = slice(first, first + piece)
                codes = codes_ref[rows, lanes].astype(jnp.float32)
                if codes_ref.dtype == jnp.int32:
                    codes = codes - MIDDLE
                mixed = offset + gain_last * codes
                for gain, half, rounder in zip(gains, halves, rounders):
                    mixed = mixed + gain * (((codes - half) + rounder) - rounder)
                out_ref[rows, lanes] = mixed.astype(jnp.bfloat16)


def serve(codes, column_block, coef, slot, source, rows_each, first_row, row_count, served):
    group_total, _, width = coef.shape
    groups = 2 if row_count > 2 * GROUP and row_count % (2 * GROUP) == 0 and first_row % (2 * GROUP) == 0 else 1
    block = groups * GROUP
    first_block = first_row // block
    steps = rows_each // block
    where = jnp.stack([source, column_block])
    whole_codes = codes.shape[0] != row_count or codes.shape[1] != width
    code_first = first_block if whole_codes else 0
    before = [] if served is None else [served]
    return pl.pallas_call(
        functools.partial(serve_kernel, groups),
        out_shape=jax.ShapeDtypeStruct((group_total * GROUP, width), jnp.bfloat16),
        grid_spec=pltpu.PrefetchScalarGridSpec(
            num_scalar_prefetch=1,
            grid=(row_count // block,),
            in_specs=[
                pl.BlockSpec((block, width), lambda i, where: (code_first + i, where[1])),
                pl.BlockSpec((groups, 8, width), lambda i, where: (slot * steps + first_block + i, 0, 0)),
            ] + [ANY] * len(before),
            out_specs=pl.BlockSpec((block, width), lambda i, where: (where[0] * steps + first_block + i, 0)),
        ),
        input_output_aliases={3: 0} if before else {},
        compiler_params=params_of(),
        cost_estimate=SMALL,
        name="serve",
    )(where, codes, coef, *before)


def local(tokens, grid_codes, residue, tile_spans, tile_scales, other_bits):
    dp_count, mp_count = lax.axis_size("dp"), lax.axis_size("mp")
    me = lax.axis_index("mp").astype(jnp.int32)
    none = jnp.int32(0)
    rows, columns = grid_codes.shape
    width = columns // mp_count
    group_count, tile_count = tile_spans.shape
    group_total = group_count * mp_count
    token_total = tokens.shape[0] * dp_count

    def shifted(value, shift):
        return lax.ppermute(value, "mp", [(z, (z + shift) % mp_count) for z in range(mp_count)])

    def cast(shift, first_row, row_count, after):
        return codes_for(grid_codes, lax.rem(me + shift, mp_count), width, first_row, row_count, after)

    shifts = sorted(range(1, mp_count), key=lambda k: -min(k, mp_count - k))
    loads = [min(k, mp_count - k) for k in shifts]
    early = max(1, sum(1 for i in range(len(shifts)) if 2 * sum(loads[:i]) < sum(loads)))
    whole = [(shift, 0, rows) for shift in shifts]
    first_parts, second_parts = whole[:early], whole[early:]
    if group_count % 8 == 0 and len(second_parts) > 1:
        last = second_parts.pop()[0]
        cut, short = rows // 2, rows // 8
        second_parts += [(last, 0, cut), (last, cut, cut - short), (last, rows - short, short)]

    arrived = []
    gram = None
    for part in first_parts:
        sent = cast(*part, [] if gram is None else [gram])
        if gram is None:
            gram = gram_blocks(tokens, [sent])
        arrived.append(shifted(sent, part[0]))

    hessian = lax.psum(gram, "dp")
    table = error_table(hessian, grid_codes, residue, tile_spans, tile_scales, token_total)
    ready = [cast(*part, [table]) for part in second_parts]
    crossing = once_there(table, ready[:1])
    tables = [table] + [shifted(crossing, shift) for shift in range(1, mp_count)]
    line = once_there(jnp.concatenate(tables), arrived)
    line_rows = line.shape[0]
    late = []
    for place, (part, sent) in enumerate(zip(second_parts, ready)):
        after = [tables[1:], arrived, late[:1]][min(place, 2)]
        late.append(shifted(once_there(sent, after), part[0]))

    line = jnp.pad(line, ((0, max(0, 64 - line_rows)), (0, 0), (0, 0)))
    gathered = lax.all_gather(line, "dp")
    goal = TARGET_BITS * (OTHER + 1) * TILES - jnp.sum(other_bits).astype(jnp.float32)
    places = jnp.stack([lax.axis_index("dp").astype(jnp.int32), me])
    pack = packed_groups(group_count, tile_count)
    coef, bits = find_slope(goal, places, gathered, line_rows, pack, tile_count, width)
    coef = coef.reshape(group_total, 8, width)
    tile_bits = bits[:group_count // pack].reshape(group_count, -1)[:, :tile_count]

    if width % 128:
        own = cast(0, 0, rows, [])
        served = serve(own, none, coef, 0, me, rows, 0, rows, None)
    else:
        served = serve(grid_codes, me, coef, 0, me, rows, 0, rows, None)
    for (shift, first_row, row_count), codes in zip(first_parts + second_parts, arrived + late):
        source = lax.rem(me + mp_count - shift, mp_count)
        served = serve(codes, none, coef, shift, source, rows, first_row, row_count, served)
    return (served, tile_bits)


def solution(mesh):
    placed = (P("dp", "mp"), P("mp", "dp"), P("mp", "dp"), P("mp", "dp"), P("mp", "dp"), P())
    return jax.shard_map(
        local,
        mesh=mesh,
        in_specs=placed,
        out_specs=(P(None, ("dp", "mp")), P("mp", "dp")),
        check_vma=False,
    )
```

```python
import functools
import math

import jax
import jax.numpy as jnp
from jax import lax
from jax.experimental import pallas as pl
from jax.experimental.pallas import tpu as pltpu
from jax.sharding import PartitionSpec as P

GROUP = 128
TRIALS = 24
OTHER = 8
TILES = 14336


BIT_WIDTHS = (2, 3, 4, 8)
ERR_WEIGHT = 16.0
SOFTMAX_WARMTH = 0.03
SLOPE_LIMIT = 16.0
TARGET_BITS = 3.5
MIDDLE = 127.5
ROUNDER = 1.5 * 2.0 ** 23
VMEM_LIMIT = 48 * 1024 * 1024

SMALL = pl.CostEstimate(flops=1000, bytes_accessed=1000, transcendentals=0)
ANY = pl.BlockSpec(memory_space=pl.ANY)
SCALARS = pl.BlockSpec(memory_space=pltpu.SMEM)


def params_of():
    return pltpu.CompilerParams(vmem_limit_bytes=VMEM_LIMIT)


def largest_divisor(total, limit, unit):
    best = unit
    for size in range(unit, limit + 1, unit):
        if total % size == 0:
            best = size
    return best


def touch_kernel(*refs):
    pass


def once_there(value, after):
    return pl.pallas_call(
        touch_kernel,
        out_shape=jax.ShapeDtypeStruct(value.shape, value.dtype),
        in_specs=[ANY] * (1 + len(after)),
        out_specs=ANY,
        input_output_aliases={0: 0},
        compiler_params=params_of(),
        cost_estimate=SMALL,
        name="once_there",
    )(value, *after)


def cast_kernel(reads, where_ref, *refs):
    out_ref = refs[-1]
    for place, codes_ref in enumerate(refs[:reads]):
        block = codes_ref.shape[0]
        centred = codes_ref[...].astype(jnp.float32) - MIDDLE
        out_ref[place * block:(place + 1) * block, :] = centred.astype(jnp.bfloat16)


def codes_for(grid_codes, dest, width, first_row, row_count, after):
    if width % 128:
        part = lax.dynamic_slice(grid_codes, (jnp.int32(first_row), dest * width), (row_count, width))
        return (part.astype(jnp.float32) - MIDDLE).astype(jnp.bfloat16)
    reads = 4
    block = largest_divisor(math.gcd(row_count // reads, first_row), GROUP, GROUP // reads)
    first_block = first_row // block

    def read(place):
        return pl.BlockSpec((block, width), lambda i, where: (first_block + i * reads + place, where[0]))

    return pl.pallas_call(
        functools.partial(cast_kernel, reads),
        out_shape=jax.ShapeDtypeStruct((row_count, width), jnp.bfloat16),
        grid_spec=pltpu.PrefetchScalarGridSpec(
            num_scalar_prefetch=1,
            grid=(row_count // (reads * block),),
            in_specs=[read(place) for place in range(reads)] + [ANY] * len(after),
            out_specs=pl.BlockSpec((reads * block, width), lambda i, where: (i, 0)),
        ),
        compiler_params=params_of(),
        cost_estimate=SMALL,
        name="cast_codes",
    )(dest.reshape(1), *[grid_codes] * reads, *after)


def gram_kernel(tokens_ref, *rest):
    out_ref = rest[-1]
    feats = tokens_ref[...]
    out_ref[0] = lax.dot_general(feats, feats, (((0,), (0,)), ((), ())), preferred_element_type=jnp.float32)


def gram_blocks(tokens, after):
    tok_count, width_local = tokens.shape
    group_count = width_local // GROUP
    return pl.pallas_call(
        gram_kernel,
        out_shape=jax.ShapeDtypeStruct((group_count, GROUP, GROUP), jnp.float32),
        grid=(group_count,),
        in_specs=[pl.BlockSpec((tok_count, GROUP), lambda g: (0, g))] + [ANY] * len(after),
        out_specs=pl.BlockSpec((1, GROUP, GROUP), lambda g: (g, 0, 0)),
        compiler_params=params_of(),
        cost_estimate=SMALL,
        name="gram",
    )(tokens, *after)


def table_kernel(token_total, chunk, pack, spans_ref, hessian_ref, codes_ref, residue_ref, factor_ref, added_ref, out_ref, sums_ref):
    group = pl.program_id(0)
    width = codes_ref.shape[1]
    tile_count = width // GROUP
    per_chunk = chunk // GROUP
    hessian = hessian_ref[0] / token_total
    high = hessian.astype(jnp.bfloat16)
    high_f = high.astype(jnp.float32)
    low = (hessian - high_f).astype(jnp.bfloat16)
    both = jnp.concatenate([high, low], axis=1)
    half_rows = 0.5 * jnp.sum(high_f + low.astype(jnp.float32), axis=1, keepdims=True)
    sums_ref[...] = jnp.zeros_like(sums_ref)

    def weigh(values):
        return jnp.dot(both, jnp.concatenate([values, values], axis=0), preferred_element_type=jnp.float32)

    def one_chunk(index, carry):
        start = pl.multiple_of(index * chunk, chunk)
        codes = codes_ref[:, pl.ds(start, chunk)]
        rest = residue_ref[:, pl.ds(start, chunk)]
        rest_weighted = weigh(rest) - half_rows
        rest_centred = rest.astype(jnp.float32) - 0.5
        spans = [spans_ref[group, index * per_chunk + t] for t in range(per_chunk)]
        for row, bit_width in enumerate(BIT_WIDTHS[:-1]):
            pieces = []
            for t in range(per_chunk):
                mask = jnp.right_shift(spans[t], bit_width) - 1
                inside = jnp.bitwise_and(codes[:, t * GROUP:(t + 1) * GROUP], mask)
                pieces.append(inside.astype(jnp.float32) - 0.5 * mask.astype(jnp.float32))
            offset = jnp.concatenate(pieces, axis=1)
            weighted = weigh(offset.astype(jnp.bfloat16)) + rest_weighted
            sums_ref[row:row + 1, pl.ds(start, chunk)] = jnp.sum((offset + rest_centred) * weighted, axis=0, keepdims=True)
        last = len(BIT_WIDTHS) - 1
        sums_ref[last:last + 1, pl.ds(start, chunk)] = jnp.sum(rest_centred * rest_weighted, axis=0, keepdims=True)
        return carry

    lax.fori_loop(0, width // chunk, one_chunk, 0)
    lanes = lax.broadcasted_iota(jnp.int32, out_ref.shape[1:], 1)
    totals = jnp.zeros(out_ref.shape[1:], jnp.float32)
    for tile in range(tile_count):
        total = jnp.sum(sums_ref[:, tile * GROUP:(tile + 1) * GROUP], axis=1, keepdims=True)
        totals = jnp.where(lanes == tile, total, totals)
    place = lax.rem(group, pack)

    @pl.when(place == 0)
    def _():
        out_ref[...] = jnp.zeros_like(out_ref)

    pitch = out_ref.shape[2] // pack
    out_ref[0] += pltpu.roll(totals * factor_ref[0] + added_ref[0], place * pitch, 1)


def packed_groups(group_count, tile_count):
    return 4 if tile_count <= 32 and group_count % 4 == 0 else 1


def error_table(hessian, grid_codes, residue, tile_spans, tile_scales, token_total):
    group_count, tile_count = tile_spans.shape
    width = grid_codes.shape[1]
    chunk = 256 if width % 256 == 0 else GROUP
    lanes = -(-tile_count // 128) * 128
    pack = packed_groups(group_count, tile_count)
    bit_count = len(BIT_WIDTHS)
    unit = tile_scales / 128.0
    factor = jnp.broadcast_to((unit * unit / float(GROUP * GROUP))[:, None, :], (group_count, bit_count, tile_count))
    factor = jnp.pad(factor, ((0, 0), (0, 8 - bit_count), (0, lanes - tile_count)))
    added = jnp.stack([tile_spans.astype(jnp.float32), tile_scales], axis=1)
    added = jnp.pad(added, ((0, 0), (bit_count, 6 - bit_count), (0, lanes - tile_count)))
    rows = pl.BlockSpec((1, 8, lanes), lambda g, spans: (g, 0, 0))
    return pl.pallas_call(
        functools.partial(table_kernel, float(token_total), chunk, pack),
        out_shape=jax.ShapeDtypeStruct((group_count // pack, 8, lanes), jnp.float32),
        grid_spec=pltpu.PrefetchScalarGridSpec(
            num_scalar_prefetch=1,
            grid=(group_count,),
            in_specs=[
                pl.BlockSpec((1, GROUP, GROUP), lambda g, spans: (g, 0, 0)),
                pl.BlockSpec((GROUP, width), lambda g, spans: (g, 0)),
                pl.BlockSpec((GROUP, width), lambda g, spans: (g, 0)),
                rows,
                rows,
            ],
            out_specs=pl.BlockSpec((1, 8, lanes), lambda g, spans: (g // pack, 0, 0)),
            scratch_shapes=[pltpu.VMEM((8, width), jnp.float32)],
        ),
        compiler_params=params_of(),
        cost_estimate=SMALL,
        name="error_table",
    )(tile_spans, hessian, grid_codes, residue, factor, added)


def probs_of(tables, slope_now):
    scores = [-(ERR_WEIGHT * t + slope_now * float(b)) / SOFTMAX_WARMTH for t, b in zip(tables, BIT_WIDTHS)]
    top = functools.reduce(jnp.maximum, scores)
    raised = [jnp.exp(score - top) for score in scores]
    total = functools.reduce(jnp.add, raised)
    return raised, total


def bits_of(tables, slope_now):
    raised, total = probs_of(tables, slope_now)
    return functools.reduce(jnp.add, [r * float(b) for r, b in zip(raised, BIT_WIDTHS)]) / total


def slope_kernel(tile_count, pack, goal_ref, me_ref, all_ref, coef_ref, bits_ref, tables_ref):
    bit_count = len(BIT_WIDTHS)
    line_count, _, _, lanes = all_ref.shape
    pitch = lanes // pack
    line_rows = bits_ref.shape[0]
    for row in range(bit_count):
        for line in range(line_count):
            tables_ref[row, line * line_rows:(line + 1) * line_rows, :] = all_ref[line, :line_rows, row, :]
    goal = goal_ref[0]
    lane = lax.broadcasted_iota(jnp.int32, tables_ref.shape[1:], 1)
    held = lax.rem(lane, jnp.int32(pitch)) < tile_count

    def trial(index, bounds):
        lower, upper = bounds
        middle = 0.5 * (lower + upper)
        bits = bits_of([tables_ref[row] for row in range(bit_count)], middle)
        above = jnp.sum(jnp.where(held, bits, 0.0)) > goal
        return (jnp.where(above, middle, lower), jnp.where(above, upper, middle))

    lower, upper = lax.fori_loop(0, TRIALS, trial, (jnp.float32(0.0), jnp.float32(SLOPE_LIMIT)))
    slope_final = 0.5 * (lower + upper)

    width = coef_ref.shape[3]
    tables = [all_ref[me_ref[0], :line_rows, row, :] for row in range(bit_count)]
    spans, scales = [all_ref[me_ref[0], :line_rows, row, :] for row in range(bit_count, bit_count + 2)]
    bits_ref[...] = bits_of(tables, slope_final)
    raised, total = probs_of(tables, slope_final)
    unit = scales / 128.0
    offset = jnp.zeros_like(unit)
    gains = []
    steps = []
    for weight, bit_width in zip(raised[:-1], BIT_WIDTHS):
        step = jnp.maximum(spans * (0.5 ** bit_width), 1.0)
        gains.append(unit * (weight / total))
        steps.append(step)
        offset = offset + gains[-1] * (0.5 * step)
    rows = [unit * (raised[-1] / total), offset] + gains + steps
    stacked = jnp.concatenate(rows, axis=0)
    lane = lax.broadcasted_iota(jnp.int32, (lanes, width), 0)
    column = lax.broadcasted_iota(jnp.int32, (lanes, width), 1) + me_ref[1] * width
    for place in range(pack):
        first = (lane - place * pitch) * GROUP
        spread = jnp.where((column >= first) & (column < first + GROUP), 1.0, 0.0)
        columns = jnp.dot(stacked, spread, precision=lax.Precision.HIGHEST, preferred_element_type=jnp.float32)
        for row in range(len(rows)):
            coef_ref[:, place, row, :] = columns[row * line_rows:(row + 1) * line_rows]


def find_slope(goal, me, gathered, line_rows, pack, tile_count, width):
    line_count, _, _, lanes = gathered.shape
    whole = pl.BlockSpec(memory_space=pltpu.VMEM)
    return pl.pallas_call(
        functools.partial(slope_kernel, tile_count, pack),
        out_shape=(
            jax.ShapeDtypeStruct((line_rows, pack, 8, width), jnp.float32),
            jax.ShapeDtypeStruct((line_rows, lanes), jnp.float32),
        ),
        in_specs=[SCALARS, SCALARS, whole],
        out_specs=(whole, whole),
        scratch_shapes=[pltpu.VMEM((len(BIT_WIDTHS), line_count * line_rows, lanes), jnp.float32)],
        compiler_params=params_of(),
        cost_estimate=SMALL,
        name="find_slope",
    )(goal.reshape(1), me, gathered)


def serve_kernel(groups, where_ref, codes_ref, coef_ref, *rest):
    out_ref = rest[-1]
    width = out_ref.shape[1]
    piece = 32
    for group in range(groups):
        for start in range(0, width, 128):
            lanes = slice(start, min(start + 128, width))
            gain_last, offset = coef_ref[group, 0:1, lanes], coef_ref[group, 1:2, lanes]
            gains = [coef_ref[group, 2 + row:3 + row, lanes] for row in range(len(BIT_WIDTHS) - 1)]
            steps = [coef_ref[group, 5 + row:6 + row, lanes] for row in range(len(BIT_WIDTHS) - 1)]
            halves = [0.5 * step for step in steps]
            rounders = [ROUNDER * step for step in steps]
            for first in range(group * GROUP, (group + 1) * GROUP, piece):
                rows = slice(first, first + piece)
                codes = codes_ref[rows, lanes].astype(jnp.float32)
                if codes_ref.dtype == jnp.int32:
                    codes = codes - MIDDLE
                mixed = offset + gain_last * codes
                for gain, half, rounder in zip(gains, halves, rounders):
                    mixed = mixed + gain * (((codes - half) + rounder) - rounder)
                out_ref[rows, lanes] = mixed.astype(jnp.bfloat16)


def serve(codes, column_block, coef, slot, source, rows_each, first_row, row_count, served):
    group_total, _, width = coef.shape
    groups = 2 if row_count > 2 * GROUP and row_count % (2 * GROUP) == 0 and first_row % (2 * GROUP) == 0 else 1
    block = groups * GROUP
    first_block = first_row // block
    steps = rows_each // block
    where = jnp.stack([source, column_block])
    whole_codes = codes.shape[0] != row_count or codes.shape[1] != width
    code_first = first_block if whole_codes else 0
    before = [] if served is None else [served]
    return pl.pallas_call(
        functools.partial(serve_kernel, groups),
        out_shape=jax.ShapeDtypeStruct((group_total * GROUP, width), jnp.bfloat16),
        grid_spec=pltpu.PrefetchScalarGridSpec(
            num_scalar_prefetch=1,
            grid=(row_count // block,),
            in_specs=[
                pl.BlockSpec((block, width), lambda i, where: (code_first + i, where[1])),
                pl.BlockSpec((groups, 8, width), lambda i, where: (slot * steps + first_block + i, 0, 0)),
            ] + [ANY] * len(before),
            out_specs=pl.BlockSpec((block, width), lambda i, where: (where[0] * steps + first_block + i, 0)),
        ),
        input_output_aliases={3: 0} if before else {},
        compiler_params=params_of(),
        cost_estimate=SMALL,
        name="serve",
    )(where, codes, coef, *before)


def local(tokens, grid_codes, residue, tile_spans, tile_scales, other_bits):
    dp_count, mp_count = lax.axis_size("dp"), lax.axis_size("mp")
    me = lax.axis_index("mp").astype(jnp.int32)
    none = jnp.int32(0)
    rows, columns = grid_codes.shape
    width = columns // mp_count
    group_count, tile_count = tile_spans.shape
    group_total = group_count * mp_count
    token_total = tokens.shape[0] * dp_count

    def shifted(value, shift):
        return lax.ppermute(value, "mp", [(z, (z + shift) % mp_count) for z in range(mp_count)])

    def cast(shift, first_row, row_count, after):
        return codes_for(grid_codes, lax.rem(me + shift, mp_count), width, first_row, row_count, after)

    shifts = sorted(range(1, mp_count), key=lambda k: -min(k, mp_count - k))
    loads = [min(k, mp_count - k) for k in shifts]
    early = max(1, sum(1 for i in range(len(shifts)) if 2 * sum(loads[:i]) < sum(loads)))
    whole = [(shift, 0, rows) for shift in shifts]
    first_parts, second_parts = whole[:early], whole[early:]
    if group_count % 8 == 0 and len(second_parts) > 1:
        last = second_parts.pop()[0]
        cut, short = rows // 2, rows // 8
        second_parts += [(last, 0, cut), (last, cut, cut - short), (last, rows - short, short)]

    arrived = []
    gram = None
    for part in first_parts:
        sent = cast(*part, [] if gram is None else [gram])
        if gram is None:
            gram = gram_blocks(tokens, [sent])
        arrived.append(shifted(sent, part[0]))

    hessian = lax.psum(gram, "dp")
    table = error_table(hessian, grid_codes, residue, tile_spans, tile_scales, token_total)
    ready = [cast(*part, [table]) for part in second_parts]
    crossing = once_there(table, ready)
    tables = [table] + [shifted(crossing, shift) for shift in range(1, mp_count)]
    line = once_there(jnp.concatenate(tables), arrived)
    line_rows = line.shape[0]
    late = []
    for place, (part, sent) in enumerate(zip(second_parts, ready)):
        if place == 1:
            sent = once_there(sent, arrived + tables[1:])
        elif place > 1:
            sent = once_there(sent, late[:1])
        late.append(shifted(sent, part[0]))

    line = jnp.pad(line, ((0, max(0, 64 - line_rows)), (0, 0), (0, 0)))
    gathered = lax.all_gather(line, "dp")
    goal = TARGET_BITS * (OTHER + 1) * TILES - jnp.sum(other_bits).astype(jnp.float32)
    places = jnp.stack([lax.axis_index("dp").astype(jnp.int32), me])
    pack = packed_groups(group_count, tile_count)
    coef, bits = find_slope(goal, places, gathered, line_rows, pack, tile_count, width)
    coef = coef.reshape(group_total, 8, width)
    tile_bits = bits[:group_count // pack].reshape(group_count, -1)[:, :tile_count]

    if width % 128:
        own = cast(0, 0, rows, [])
        served = serve(own, none, coef, 0, me, rows, 0, rows, None)
    else:
        served = serve(grid_codes, me, coef, 0, me, rows, 0, rows, None)
    for (shift, first_row, row_count), codes in zip(first_parts + second_parts, arrived + late):
        source = lax.rem(me + mp_count - shift, mp_count)
        served = serve(codes, none, coef, shift, source, rows, first_row, row_count, served)
    return (served, tile_bits)


def solution(mesh):
    placed = (P("dp", "mp"), P("mp", "dp"), P("mp", "dp"), P("mp", "dp"), P("mp", "dp"), P())
    return jax.shard_map(
        local,
        mesh=mesh,
        in_specs=placed,
        out_specs=(P(None, ("dp", "mp")), P("mp", "dp")),
        check_vma=False,
    )
```

```python
import functools
import math

import jax
import jax.numpy as jnp
from jax import lax
from jax.experimental import pallas as pl
from jax.experimental.pallas import tpu as pltpu
from jax.sharding import PartitionSpec as P

GROUP = 128
TRIALS = 24
OTHER = 8
TILES = 14336


BIT_WIDTHS = (2, 3, 4, 8)
ERR_WEIGHT = 16.0
SOFTMAX_WARMTH = 0.03
SLOPE_LIMIT = 16.0
TARGET_BITS = 3.5
MIDDLE = 127.5
ROUNDER = 1.5 * 2.0 ** 23
VMEM_LIMIT = 48 * 1024 * 1024

SMALL = pl.CostEstimate(flops=1000, bytes_accessed=1000, transcendentals=0)
ANY = pl.BlockSpec(memory_space=pl.ANY)
SCALARS = pl.BlockSpec(memory_space=pltpu.SMEM)


def params_of():
    return pltpu.CompilerParams(vmem_limit_bytes=VMEM_LIMIT)


def largest_divisor(total, limit, unit):
    best = unit
    for size in range(unit, limit + 1, unit):
        if total % size == 0:
            best = size
    return best


def touch_kernel(*refs):
    pass


def once_there(value, after):
    return pl.pallas_call(
        touch_kernel,
        out_shape=jax.ShapeDtypeStruct(value.shape, value.dtype),
        in_specs=[ANY] * (1 + len(after)),
        out_specs=ANY,
        input_output_aliases={0: 0},
        compiler_params=params_of(),
        cost_estimate=SMALL,
        name="once_there",
    )(value, *after)


def cast_kernel(reads, where_ref, *refs):
    out_ref = refs[-1]
    for place, codes_ref in enumerate(refs[:reads]):
        block = codes_ref.shape[0]
        centred = codes_ref[...].astype(jnp.float32) - MIDDLE
        out_ref[place * block:(place + 1) * block, :] = centred.astype(jnp.bfloat16)


def codes_for(grid_codes, dest, width, first_row, row_count, after):
    if width % 128:
        part = lax.dynamic_slice(grid_codes, (jnp.int32(first_row), dest * width), (row_count, width))
        return (part.astype(jnp.float32) - MIDDLE).astype(jnp.bfloat16)
    reads = 4
    block = largest_divisor(math.gcd(row_count // reads, first_row), GROUP // 2, GROUP // reads)
    first_block = first_row // block

    def read(place):
        return pl.BlockSpec((block, width), lambda i, where: (first_block + i * reads + place, where[0]))

    return pl.pallas_call(
        functools.partial(cast_kernel, reads),
        out_shape=jax.ShapeDtypeStruct((row_count, width), jnp.bfloat16),
        grid_spec=pltpu.PrefetchScalarGridSpec(
            num_scalar_prefetch=1,
            grid=(row_count // (reads * block),),
            in_specs=[read(place) for place in range(reads)] + [ANY] * len(after),
            out_specs=pl.BlockSpec((reads * block, width), lambda i, where: (i, 0)),
        ),
        compiler_params=params_of(),
        cost_estimate=SMALL,
        name="cast_codes",
    )(dest.reshape(1), *[grid_codes] * reads, *after)


def gram_kernel(tokens_ref, *rest):
    out_ref = rest[-1]
    feats = tokens_ref[...]
    out_ref[0] = lax.dot_general(feats, feats, (((0,), (0,)), ((), ())), preferred_element_type=jnp.float32)


def gram_blocks(tokens, after):
    tok_count, width_local = tokens.shape
    group_count = width_local // GROUP
    return pl.pallas_call(
        gram_kernel,
        out_shape=jax.ShapeDtypeStruct((group_count, GROUP, GROUP), jnp.float32),
        grid=(group_count,),
        in_specs=[pl.BlockSpec((tok_count, GROUP), lambda g: (0, g))] + [ANY] * len(after),
        out_specs=pl.BlockSpec((1, GROUP, GROUP), lambda g: (g, 0, 0)),
        compiler_params=params_of(),
        cost_estimate=SMALL,
        name="gram",
    )(tokens, *after)


def table_kernel(token_total, chunk, pack, spans_ref, hessian_ref, codes_ref, residue_ref, factor_ref, added_ref, out_ref, sums_ref):
    group = pl.program_id(0)
    width = codes_ref.shape[1]
    tile_count = width // GROUP
    per_chunk = chunk // GROUP
    hessian = hessian_ref[0] / token_total
    high = hessian.astype(jnp.bfloat16)
    high_f = high.astype(jnp.float32)
    low = (hessian - high_f).astype(jnp.bfloat16)
    both = jnp.concatenate([high, low], axis=1)
    half_rows = 0.5 * jnp.sum(high_f + low.astype(jnp.float32), axis=1, keepdims=True)
    sums_ref[...] = jnp.zeros_like(sums_ref)

    def weigh(values):
        return jnp.dot(both, jnp.concatenate([values, values], axis=0), preferred_element_type=jnp.float32)

    def one_chunk(index, carry):
        start = pl.multiple_of(index * chunk, chunk)
        codes = codes_ref[:, pl.ds(start, chunk)]
        rest = residue_ref[:, pl.ds(start, chunk)]
        rest_weighted = weigh(rest) - half_rows
        rest_centred = rest.astype(jnp.float32) - 0.5
        spans = [spans_ref[group, index * per_chunk + t] for t in range(per_chunk)]
        for row, bit_width in enumerate(BIT_WIDTHS[:-1]):
            pieces = []
            for t in range(per_chunk):
                mask = jnp.right_shift(spans[t], bit_width) - 1
                inside = jnp.bitwise_and(codes[:, t * GROUP:(t + 1) * GROUP], mask)
                pieces.append(inside.astype(jnp.float32) - 0.5 * mask.astype(jnp.float32))
            offset = jnp.concatenate(pieces, axis=1)
            weighted = weigh(offset.astype(jnp.bfloat16)) + rest_weighted
            sums_ref[row:row + 1, pl.ds(start, chunk)] = jnp.sum((offset + rest_centred) * weighted, axis=0, keepdims=True)
        last = len(BIT_WIDTHS) - 1
        sums_ref[last:last + 1, pl.ds(start, chunk)] = jnp.sum(rest_centred * rest_weighted, axis=0, keepdims=True)
        return carry

    lax.fori_loop(0, width // chunk, one_chunk, 0)
    lanes = lax.broadcasted_iota(jnp.int32, out_ref.shape[1:], 1)
    totals = jnp.zeros(out_ref.shape[1:], jnp.float32)
    for tile in range(tile_count):
        total = jnp.sum(sums_ref[:, tile * GROUP:(tile + 1) * GROUP], axis=1, keepdims=True)
        totals = jnp.where(lanes == tile, total, totals)
    place = lax.rem(group, pack)

    @pl.when(place == 0)
    def _():
        out_ref[...] = jnp.zeros_like(out_ref)

    pitch = out_ref.shape[2] // pack
    out_ref[0] += pltpu.roll(totals * factor_ref[0] + added_ref[0], place * pitch, 1)


def packed_groups(group_count, tile_count):
    return 4 if tile_count <= 32 and group_count % 4 == 0 else 1


def error_table(hessian, grid_codes, residue, tile_spans, tile_scales, token_total):
    group_count, tile_count = tile_spans.shape
    width = grid_codes.shape[1]
    chunk = 256 if width % 256 == 0 else GROUP
    lanes = -(-tile_count // 128) * 128
    pack = packed_groups(group_count, tile_count)
    bit_count = len(BIT_WIDTHS)
    unit = tile_scales / 128.0
    factor = jnp.broadcast_to((unit * unit / float(GROUP * GROUP))[:, None, :], (group_count, bit_count, tile_count))
    factor = jnp.pad(factor, ((0, 0), (0, 8 - bit_count), (0, lanes - tile_count)))
    added = jnp.stack([tile_spans.astype(jnp.float32), tile_scales], axis=1)
    added = jnp.pad(added, ((0, 0), (bit_count, 6 - bit_count), (0, lanes - tile_count)))
    rows = pl.BlockSpec((1, 8, lanes), lambda g, spans: (g, 0, 0))
    return pl.pallas_call(
        functools.partial(table_kernel, float(token_total), chunk, pack),
        out_shape=jax.ShapeDtypeStruct((group_count // pack, 8, lanes), jnp.float32),
        grid_spec=pltpu.PrefetchScalarGridSpec(
            num_scalar_prefetch=1,
            grid=(group_count,),
            in_specs=[
                pl.BlockSpec((1, GROUP, GROUP), lambda g, spans: (g, 0, 0)),
                pl.BlockSpec((GROUP, width), lambda g, spans: (g, 0)),
                pl.BlockSpec((GROUP, width), lambda g, spans: (g, 0)),
                rows,
                rows,
            ],
            out_specs=pl.BlockSpec((1, 8, lanes), lambda g, spans: (g // pack, 0, 0)),
            scratch_shapes=[pltpu.VMEM((8, width), jnp.float32)],
        ),
        compiler_params=params_of(),
        cost_estimate=SMALL,
        name="error_table",
    )(tile_spans, hessian, grid_codes, residue, factor, added)


def probs_of(tables, slope_now):
    scores = [-(ERR_WEIGHT * t + slope_now * float(b)) / SOFTMAX_WARMTH for t, b in zip(tables, BIT_WIDTHS)]
    top = functools.reduce(jnp.maximum, scores)
    raised = [jnp.exp(score - top) for score in scores]
    total = functools.reduce(jnp.add, raised)
    return raised, total


def bits_of(tables, slope_now):
    raised, total = probs_of(tables, slope_now)
    return functools.reduce(jnp.add, [r * float(b) for r, b in zip(raised, BIT_WIDTHS)]) / total


def slope_kernel(tile_count, pack, goal_ref, me_ref, all_ref, coef_ref, bits_ref, tables_ref):
    bit_count = len(BIT_WIDTHS)
    line_count, _, _, lanes = all_ref.shape
    pitch = lanes // pack
    line_rows = bits_ref.shape[0]
    for row in range(bit_count):
        for line in range(line_count):
            tables_ref[row, line * line_rows:(line + 1) * line_rows, :] = all_ref[line, :line_rows, row, :]
    goal = goal_ref[0]
    lane = lax.broadcasted_iota(jnp.int32, tables_ref.shape[1:], 1)
    held = lax.rem(lane, jnp.int32(pitch)) < tile_count

    def trial(index, bounds):
        lower, upper = bounds
        middle = 0.5 * (lower + upper)
        bits = bits_of([tables_ref[row] for row in range(bit_count)], middle)
        above = jnp.sum(jnp.where(held, bits, 0.0)) > goal
        return (jnp.where(above, middle, lower), jnp.where(above, upper, middle))

    lower, upper = lax.fori_loop(0, TRIALS, trial, (jnp.float32(0.0), jnp.float32(SLOPE_LIMIT)))
    slope_final = 0.5 * (lower + upper)

    width = coef_ref.shape[3]
    tables = [all_ref[me_ref[0], :line_rows, row, :] for row in range(bit_count)]
    spans, scales = [all_ref[me_ref[0], :line_rows, row, :] for row in range(bit_count, bit_count + 2)]
    bits_ref[...] = bits_of(tables, slope_final)
    raised, total = probs_of(tables, slope_final)
    unit = scales / 128.0
    offset = jnp.zeros_like(unit)
    gains = []
    steps = []
    for weight, bit_width in zip(raised[:-1], BIT_WIDTHS):
        step = jnp.maximum(spans * (0.5 ** bit_width), 1.0)
        gains.append(unit * (weight / total))
        steps.append(step)
        offset = offset + gains[-1] * (0.5 * step)
    rows = [unit * (raised[-1] / total), offset] + gains + steps
    stacked = jnp.concatenate(rows, axis=0)
    lane = lax.broadcasted_iota(jnp.int32, (lanes, width), 0)
    column = lax.broadcasted_iota(jnp.int32, (lanes, width), 1) + me_ref[1] * width
    for place in range(pack):
        first = (lane - place * pitch) * GROUP
        spread = jnp.where((column >= first) & (column < first + GROUP), 1.0, 0.0)
        columns = jnp.dot(stacked, spread, precision=lax.Precision.HIGHEST, preferred_element_type=jnp.float32)
        for row in range(len(rows)):
            coef_ref[:, place, row, :] = columns[row * line_rows:(row + 1) * line_rows]


def find_slope(goal, me, gathered, line_rows, pack, tile_count, width):
    line_count, _, _, lanes = gathered.shape
    whole = pl.BlockSpec(memory_space=pltpu.VMEM)
    return pl.pallas_call(
        functools.partial(slope_kernel, tile_count, pack),
        out_shape=(
            jax.ShapeDtypeStruct((line_rows, pack, 8, width), jnp.float32),
            jax.ShapeDtypeStruct((line_rows, lanes), jnp.float32),
        ),
        in_specs=[SCALARS, SCALARS, whole],
        out_specs=(whole, whole),
        scratch_shapes=[pltpu.VMEM((len(BIT_WIDTHS), line_count * line_rows, lanes), jnp.float32)],
        compiler_params=params_of(),
        cost_estimate=SMALL,
        name="find_slope",
    )(goal.reshape(1), me, gathered)


def serve_kernel(groups, where_ref, codes_ref, coef_ref, *rest):
    out_ref = rest[-1]
    width = out_ref.shape[1]
    piece = 32
    for group in range(groups):
        for start in range(0, width, 128):
            lanes = slice(start, min(start + 128, width))
            gain_last, offset = coef_ref[group, 0:1, lanes], coef_ref[group, 1:2, lanes]
            gains = [coef_ref[group, 2 + row:3 + row, lanes] for row in range(len(BIT_WIDTHS) - 1)]
            steps = [coef_ref[group, 5 + row:6 + row, lanes] for row in range(len(BIT_WIDTHS) - 1)]
            halves = [0.5 * step for step in steps]
            rounders = [ROUNDER * step for step in steps]
            for first in range(group * GROUP, (group + 1) * GROUP, piece):
                rows = slice(first, first + piece)
                codes = codes_ref[rows, lanes].astype(jnp.float32)
                if codes_ref.dtype == jnp.int32:
                    codes = codes - MIDDLE
                mixed = offset + gain_last * codes
                for gain, half, rounder in zip(gains, halves, rounders):
                    mixed = mixed + gain * (((codes - half) + rounder) - rounder)
                out_ref[rows, lanes] = mixed.astype(jnp.bfloat16)


def serve(codes, column_block, coef, slot, source, rows_each, first_row, row_count, served):
    group_total, _, width = coef.shape
    groups = 2 if row_count > 2 * GROUP and row_count % (2 * GROUP) == 0 and first_row % (2 * GROUP) == 0 else 1
    block = groups * GROUP
    first_block = first_row // block
    steps = rows_each // block
    where = jnp.stack([source, column_block])
    whole_codes = codes.shape[0] != row_count or codes.shape[1] != width
    code_first = first_block if whole_codes else 0
    before = [] if served is None else [served]
    return pl.pallas_call(
        functools.partial(serve_kernel, groups),
        out_shape=jax.ShapeDtypeStruct((group_total * GROUP, width), jnp.bfloat16),
        grid_spec=pltpu.PrefetchScalarGridSpec(
            num_scalar_prefetch=1,
            grid=(row_count // block,),
            in_specs=[
                pl.BlockSpec((block, width), lambda i, where: (code_first + i, where[1])),
                pl.BlockSpec((groups, 8, width), lambda i, where: (slot * steps + first_block + i, 0, 0)),
            ] + [ANY] * len(before),
            out_specs=pl.BlockSpec((block, width), lambda i, where: (where[0] * steps + first_block + i, 0)),
        ),
        input_output_aliases={3: 0} if before else {},
        compiler_params=params_of(),
        cost_estimate=SMALL,
        name="serve",
    )(where, codes, coef, *before)


def local(tokens, grid_codes, residue, tile_spans, tile_scales, other_bits):
    dp_count, mp_count = lax.axis_size("dp"), lax.axis_size("mp")
    me = lax.axis_index("mp").astype(jnp.int32)
    none = jnp.int32(0)
    rows, columns = grid_codes.shape
    width = columns // mp_count
    group_count, tile_count = tile_spans.shape
    group_total = group_count * mp_count
    token_total = tokens.shape[0] * dp_count

    def shifted(value, shift):
        return lax.ppermute(value, "mp", [(z, (z + shift) % mp_count) for z in range(mp_count)])

    def cast(shift, first_row, row_count, after):
        return codes_for(grid_codes, lax.rem(me + shift, mp_count), width, first_row, row_count, after)

    shifts = sorted(range(1, mp_count), key=lambda k: -min(k, mp_count - k))
    loads = [min(k, mp_count - k) for k in shifts]
    early = max(1, sum(1 for i in range(len(shifts)) if 2 * sum(loads[:i]) < sum(loads)))
    whole = [(shift, 0, rows) for shift in shifts]
    first_parts, second_parts = whole[:early], whole[early:]
    if group_count % 8 == 0 and len(second_parts) > 1:
        last = second_parts.pop()[0]
        cut, short = rows // 2, rows // 8
        second_parts += [(last, 0, cut), (last, cut, cut - short), (last, rows - short, short)]

    arrived = []
    gram = None
    for part in first_parts:
        sent = cast(*part, [] if gram is None else [gram])
        if gram is None:
            gram = gram_blocks(tokens, [sent])
        arrived.append(shifted(sent, part[0]))

    hessian = lax.psum(gram, "dp")
    table = error_table(hessian, grid_codes, residue, tile_spans, tile_scales, token_total)
    ready = [cast(*part, [table]) for part in second_parts]
    crossing = once_there(table, ready)
    tables = [table] + [shifted(crossing, shift) for shift in range(1, mp_count)]
    line = once_there(jnp.concatenate(tables), arrived)
    line_rows = line.shape[0]
    late = []
    for place, (part, sent) in enumerate(zip(second_parts, ready)):
        if place == 1:
            sent = once_there(sent, arrived + tables[1:])
        elif place > 1:
            sent = once_there(sent, late[:1])
        late.append(shifted(sent, part[0]))

    line = jnp.pad(line, ((0, max(0, 64 - line_rows)), (0, 0), (0, 0)))
    gathered = lax.all_gather(line, "dp")
    goal = TARGET_BITS * (OTHER + 1) * TILES - jnp.sum(other_bits).astype(jnp.float32)
    places = jnp.stack([lax.axis_index("dp").astype(jnp.int32), me])
    pack = packed_groups(group_count, tile_count)
    coef, bits = find_slope(goal, places, gathered, line_rows, pack, tile_count, width)
    coef = coef.reshape(group_total, 8, width)
    tile_bits = bits[:group_count // pack].reshape(group_count, -1)[:, :tile_count]

    if width % 128:
        own = cast(0, 0, rows, [])
        served = serve(own, none, coef, 0, me, rows, 0, rows, None)
    else:
        served = serve(grid_codes, me, coef, 0, me, rows, 0, rows, None)
    for (shift, first_row, row_count), codes in zip(first_parts + second_parts, arrived + late):
        source = lax.rem(me + mp_count - shift, mp_count)
        served = serve(codes, none, coef, shift, source, rows, first_row, row_count, served)
    return (served, tile_bits)


def solution(mesh):
    placed = (P("dp", "mp"), P("mp", "dp"), P("mp", "dp"), P("mp", "dp"), P("mp", "dp"), P())
    return jax.shard_map(
        local,
        mesh=mesh,
        in_specs=placed,
        out_specs=(P(None, ("dp", "mp")), P("mp", "dp")),
        check_vma=False,
    )
```
